32 devices in a mesh: lat: 4 (over y, core), lon: 8 (over z, x).
Axes of the slice: x: 2, y: 2, z: 4, core: 2. Of those that a mesh axis runs over, the one named last changes fastest.
Arguments:
- source_elements: bfloat16 [16384, 256], P(('lat', 'lon')), may hold values from -6 to 6
- remap_weights: bfloat16 [32, 32, 6, 16, 128], P(('lat', 'lon')), may hold values from -1.5 to 1.5
- element_index: int32 [32, 32, 6], P(('lat', 'lon')), may hold values from 0 to 511
- patch_index: int32 [32, 32, 6], P(('lat', 'lon')), may hold values from 0 to 127
- block_counts: int32 [32, 32], P(('lat', 'lon')), may hold values from 2 to 6, as said below
- conv_weight: bfloat16 [9, 64, 16], replicated, may hold values from -0.5 to 0.5
- cotangent: bfloat16 [64, 64, 8192], P('lat', None, 'lon'), may hold values from -6 to 6
Outputs:
- features_out: bfloat16 [64, 64, 8192], P('lat', None, 'lon')
- input_grad: bfloat16 [64, 16, 8192], P('lat', None, 'lon')
- weight_grad: float32 [9, 64, 16], replicated
The draws below stay inside these ranges and needn't reach their ends.
Inputs may be any that keep to these rules, and one draw needn't show every extreme that they name: `block_counts`: at most 6 valid slots from one device to one owner; in every draw one owner, drawn from the seed, receives exactly 6 from every device.
All inputs are finite; a program needn't handle non-finite values.
Results may differ from the reference program's by a relative error of at most 0.0058.
Values may be sent and summed in bfloat16 or wider, within the bound.
A program may use at most 128 MiB of HBM per device.

```python
import math
from functools import partial
import jax
import jax.numpy as jnp
from jax import lax

VARS = 16
C = 64
NPTS = 16
PATCH = 128
RATE = 4
CAP = 6
ROWS_DEV = 16
COLS_DEV = 1024
SRC_DEV = 512
PATCHES = 128
NROWS = 64
NCOLS = 8192
N_LAT = 4
N_LON = 8


def draw_block_counts(key, part):
    key = jax.random.fold_in(key, 7)
    first_key, second_key = jax.random.split(key)
    owner_count = N_LAT * N_LON
    heavy_owner = jax.random.randint(first_key, (), 0, owner_count)
    drawn = jax.random.randint(second_key, (owner_count, owner_count), max(1, CAP // 3), CAP + 1)
    columns = jnp.arange(owner_count)[None, :]
    return jnp.where(columns == heavy_owner, CAP, drawn).astype(jnp.int32)


def place_ends(result, stream_key, least, top_value):
    shape = result.shape
    place = [jax.random.randint(jax.random.fold_in(stream_key, axis), (), 0, shape[axis]) for axis in range(len(shape))]
    result = result.at[tuple(place)].set(least)
    longest = shape.index(max(shape))
    place[longest] = (place[longest] + 1) % shape[longest]
    return result.at[tuple(place)].set(top_value)


def shard_levels(own_key, extent, cuts, smallest, top_value):
    gain, own = 1.0, jax.random.fold_in(own_key, 6)
    for position, shards_of in cuts:
        steps = jnp.exp(jax.random.uniform(jax.random.fold_in(own, position), (shards_of,), jnp.float32, smallest / len(cuts), top_value / len(cuts)))
        gain = gain * jnp.repeat(steps, extent[position] // shards_of).reshape([-1 if axis == position else 1 for axis in range(len(extent))])
    return gain


def centred(rng, dims, width, most, pieces=(), held_as=jnp.bfloat16):
    entries = width * jax.random.normal(rng, dims, jnp.float32)
    if pieces:
        entries = entries * shard_levels(rng, dims, pieces, -0.22, 0.18)
    return jnp.clip(entries, -most, most).astype(held_as)


def setup_inputs(seed: int = 0) -> dict:
    streams_of = jax.random.split(jax.random.key(seed), 8)
    return {
        "source_elements": centred(streams_of[0], (SRC_DEV * N_LAT * N_LON, NPTS * VARS), 1.0, 6.0, ((0, 32),)),
        "remap_weights": centred(streams_of[1], (N_LAT * N_LON, N_LAT * N_LON, CAP, NPTS, PATCH), NPTS ** -0.5, 1.5, ((0, 32),)),
        "element_index": place_ends(jax.random.randint(streams_of[2], (N_LAT * N_LON, N_LAT * N_LON, CAP), 0, SRC_DEV), jax.random.fold_in(streams_of[2], 1), 0, SRC_DEV - 1).astype(jnp.int32),
        "patch_index": place_ends(jax.random.randint(streams_of[3], (N_LAT * N_LON, N_LAT * N_LON, CAP), 0, PATCHES), jax.random.fold_in(streams_of[3], 1), 0, PATCHES - 1).astype(jnp.int32),
        "block_counts": draw_block_counts(jax.random.fold_in(streams_of[7], 71), 0),
        "conv_weight": centred(streams_of[5], (9, C, VARS), (9 * VARS) ** -0.5, 0.5),
        "cotangent": centred(streams_of[6], (NROWS, C, NCOLS), 1.0, 6.0, ((0, 4), (2, 8))),
    }


def tap_offsets():
    return [((tap_number // 3 - 1) * RATE, (tap_number % 3 - 1) * RATE) for tap_number in range(9)]

def owner_field(owner_index, source_blocks, remap_weights, element_index, patch_index, block_counts):
    owner_count = N_LAT * N_LON
    weights_in = lax.dynamic_index_in_dim(remap_weights, owner_index, 1, keepdims=False).astype(jnp.float32)
    chosen = lax.dynamic_index_in_dim(element_index, owner_index, 1, keepdims=False)
    targets = lax.dynamic_index_in_dim(patch_index, owner_index, 1, keepdims=False)
    counts = lax.dynamic_index_in_dim(block_counts, owner_index, 1, keepdims=False)
    element_rows = jnp.take_along_axis(source_blocks, chosen[:, :, None], axis=1)
    element_rows = element_rows.reshape(owner_count, CAP, NPTS, VARS).astype(jnp.float32)
    blocks = jnp.einsum('skjc,skjp->skcp', element_rows, weights_in)
    live_slots = (jnp.arange(CAP, dtype=jnp.int32)[None, :] < counts[:, None]).astype(jnp.float32)
    blocks = blocks * live_slots[:, :, None, None]
    blocks = lax.optimization_barrier(blocks.astype(jnp.bfloat16)).astype(jnp.float32)
    summed = jax.ops.segment_sum(blocks.reshape(owner_count * CAP, VARS, PATCH), targets.reshape(owner_count * CAP), num_segments=PATCHES)
    remapped = summed.reshape(ROWS_DEV, COLS_DEV // PATCH, VARS, PATCH).transpose(0, 2, 1, 3)
    return remapped.reshape(ROWS_DEV, VARS, COLS_DEV).astype(jnp.bfloat16)

def conv_block(padded_x, padded_g, conv_weight):
    wide_weights = conv_weight.astype(jnp.float32)
    band_rows = padded_x.shape[0] - 2 * RATE
    band_cols = padded_x.shape[2] - 2 * RATE
    cot_rows = padded_g[RATE:RATE + band_rows, :, RATE:RATE + band_cols].astype(jnp.float32)
    forward = jnp.zeros((band_rows, C, band_cols), jnp.float32)
    backward = jnp.zeros((band_rows, VARS, band_cols), jnp.float32)
    partials = []
    for tap_number, (row_shift, col_shift) in enumerate(tap_offsets()):
        shifted = padded_x[RATE + row_shift:RATE + row_shift + band_rows, :, RATE + col_shift:RATE + col_shift + band_cols].astype(jnp.float32)
        forward = forward + jnp.einsum('oc,rcw->row', wide_weights[tap_number], shifted)
        back_piece = padded_g[RATE - row_shift:RATE - row_shift + band_rows, :, RATE - col_shift:RATE - col_shift + band_cols].astype(jnp.float32)
        backward = backward + jnp.einsum('oc,row->rcw', wide_weights[tap_number], back_piece)
        partials.append(jnp.einsum('row,rcw->oc', cot_rows, shifted))
    return (forward.astype(jnp.bfloat16), backward.astype(jnp.bfloat16), jnp.stack(partials))

def pad_band(values):
    wrapped = jnp.concatenate([values[:, :, -RATE:], values, values[:, :, :RATE]], axis=2)
    return jnp.pad(wrapped, ((RATE, RATE), (0, 0), (0, 0)))

def reference(source_elements, remap_weights, element_index, patch_index, block_counts, conv_weight, cotangent):
    owner_count = N_LAT * N_LON
    source_blocks = source_elements.reshape(owner_count, SRC_DEV, NPTS * VARS)
    owner_tiles = lax.map(partial(owner_field, source_blocks=source_blocks, remap_weights=remap_weights, element_index=element_index, patch_index=patch_index, block_counts=block_counts), jnp.arange(owner_count, dtype=jnp.int32))
    remapped = owner_tiles.reshape(N_LAT, N_LON, ROWS_DEV, VARS, COLS_DEV).transpose(0, 2, 3, 1, 4).reshape(NROWS, VARS, NCOLS)
    padded_x = pad_band(remapped)
    padded_g = pad_band(cotangent)

    def one_band(band_index):
        row_start = band_index * ROWS_DEV
        band_x = lax.dynamic_slice_in_dim(padded_x, row_start, ROWS_DEV + 2 * RATE, 0)
        band_g = lax.dynamic_slice_in_dim(padded_g, row_start, ROWS_DEV + 2 * RATE, 0)
        return conv_block(band_x, band_g, conv_weight)
    forward, backward, partials = lax.map(one_band, jnp.arange(N_LAT, dtype=jnp.int32))
    features_out = forward.reshape(NROWS, C, NCOLS)
    input_grad = backward.reshape(NROWS, VARS, NCOLS)
    weight_grad = lax.optimization_barrier(jnp.sum(partials, axis=0)) / math.sqrt(NROWS * NCOLS)
    return (features_out, input_grad, weight_grad)
```

```python
import functools
import math

import jax
import jax.numpy as jnp
from jax import lax
from jax.experimental import pallas as pl
from jax.experimental.pallas import tpu as pltpu
from jax.sharding import PartitionSpec as P

RATE = 4
EDGE = 128
MESH = pl.DeviceIdType.MESH
F32 = jnp.float32
BF16 = jnp.bfloat16
SIDES = [(-1, -1), (-1, 0), (-1, 1), (0, -1), (0, 1), (1, -1), (1, 0), (1, 1)]


def span(step, total, width):
    before, size = width
    if step < 0:
        return (0, size), (before + total, size)
    if step > 0:
        return (total - size, size), (before - size, size)
    return (0, total), (before, total)


def halo_copies(field, padded, send, recv, nlat, nlon):
    lat, lon = lax.axis_index("lat"), lax.axis_index("lon")
    rows, _, cols = field.shape
    made = []
    for k, (dr, dc) in enumerate(SIDES):
        (r0, rn), (pr, _) = span(dr, rows, (RATE, RATE))
        (c0, cn), (pc, _) = span(dc, cols, (EDGE, EDGE))
        to_lat, from_lat = lat + dr, lat - dr
        copy = pltpu.make_async_remote_copy(
            src_ref=field.at[pl.ds(r0, rn), :, pl.ds(c0, cn)],
            dst_ref=padded.at[pl.ds(pr, rn), :, pl.ds(pc, cn)],
            send_sem=send.at[k],
            recv_sem=recv.at[k],
            device_id=(lax.rem(to_lat + nlat, nlat), lax.rem(lon + dc + nlon, nlon)),
            device_id_type=MESH,
        )
        sends = (to_lat >= 0) & (to_lat < nlat)
        gets = (from_lat >= 0) & (from_lat < nlat)
        made.append((dr, sends, gets, copy))
    return made


def halo_do(made, what):
    for dr, sends, gets, copy in made:
        cond = gets if what == "wait_recv" else sends
        act = getattr(copy, what)
        if dr == 0:
            act()
        else:
            pl.when(cond)(act)


def zero_border(padded, rows, nlat):
    lat = lax.axis_index("lat")

    @pl.when(lat == 0)
    def _():
        padded[0:RATE] = jnp.zeros((RATE,) + padded.shape[1:], padded.dtype)

    @pl.when(lat == nlat - 1)
    def _():
        padded[RATE + rows : 2 * RATE + rows] = jnp.zeros(
            (RATE,) + padded.shape[1:], padded.dtype
        )


def exchange_kernel(
    nlat, nlon, pay, tgt, g, wb, arr, tarr, ig, gp, psend, precv, tsend, trecv, hsend, hrecv, lsem
):
    lat, lon = lax.axis_index("lat"), lax.axis_index("lon")
    n = nlat * nlon
    me = lat * nlon + lon
    rows, _, cols = g.shape
    nvars = ig.shape[1]
    zero_border(gp, rows, nlat)
    own_g = pltpu.make_async_copy(
        g, gp.at[pl.ds(RATE, rows), :, pl.ds(EDGE, cols)], lsem.at[0]
    )
    own_g.start()
    own_p = pltpu.make_async_copy(pay.at[me], arr.at[me], lsem.at[1])
    own_t = pltpu.make_async_copy(tgt.at[me], tarr.at[me], lsem.at[2])
    own_p.start()
    own_t.start()

    barrier = pltpu.get_barrier_semaphore()

    def greet(i, carry):
        peer = lax.rem(me + i, n)
        pl.semaphore_signal(
            barrier, inc=1, device_id=(peer // nlon, lax.rem(peer, nlon)), device_id_type=MESH
        )
        return carry

    lax.fori_loop(1, n, greet, 0)
    pl.semaphore_wait(barrier, n - 1)

    def block(i, forward):
        peer = lax.rem(me + i, n) if forward else lax.rem(me + n - i, n)
        slot = me if forward else peer
        where = (peer // nlon, lax.rem(peer, nlon))
        return (
            pltpu.make_async_remote_copy(
                pay.at[peer], arr.at[slot], psend.at[i], precv.at[slot],
                device_id=where, device_id_type=MESH,
            ),
            pltpu.make_async_remote_copy(
                tgt.at[peer], tarr.at[slot], tsend.at[i], trecv.at[slot],
                device_id=where, device_id_type=MESH,
            ),
        )

    halo = halo_copies(g, gp, hsend, hrecv, nlat, nlon)

    def send(i, carry):
        data, number = block(i, True)
        number.start()
        data.start()
        return carry

    lax.fori_loop(1, n, send, 0)
    halo_do(halo, "start")
    own_g.wait()
    halo_do(halo, "wait_recv")

    def back(r, carry):
        stack = jnp.concatenate([gp[r + 2 * RATE], gp[r + RATE], gp[r]], axis=0)
        y = jnp.dot(wb[...], stack, preferred_element_type=F32)
        width = cols + 2 * EDGE
        low = pltpu.roll(y[0:nvars], width - RATE, 1)
        high = pltpu.roll(y[2 * nvars : 3 * nvars], RATE, 1)
        total = low + y[nvars : 2 * nvars] + high
        ig[r] = total[:, EDGE : EDGE + cols].astype(BF16)
        return carry

    lax.fori_loop(0, rows, back, 0)
    halo_do(halo, "wait_send")
    own_p.wait()
    own_t.wait()

    def finish(i, carry):
        data, number = block(i, False)
        number.wait_recv()
        data.wait_recv()
        number.wait_send()
        data.wait_send()
        return carry

    lax.fori_loop(1, n, finish, 0)


def scatter_kernel(cap, tgt, arr, x, acc):
    n = arr.shape[0]
    rows, nvars, cols = x.shape
    across = cols // EDGE
    acc[...] = jnp.zeros_like(acc)

    def add(s, carry):
        for j in range(cap):
            q = tgt[s, 0, j]
            acc[q] = acc[q] + arr[s, j * nvars : (j + 1) * nvars, :].astype(F32)
        return carry

    lax.fori_loop(0, n, add, 0)

    def store(r, carry):
        for c in range(across):
            x[r, :, c * EDGE : (c + 1) * EDGE] = acc[r * across + c].astype(BF16)
        return carry

    lax.fori_loop(0, rows, store, 0)


def conv_kernel(
    nlat, nlon, scale, x, g, wf, feat, dw,
    xp, xs, gv, acc, latbuf, part, lonbuf, done,
    hsend, hrecv, asend, arecv, bsend, brecv, csend, crecv, lsem,
):
    lat, lon = lax.axis_index("lat"), lax.axis_index("lon")
    rows, nvars, cols = x.shape
    outs = g.shape[1]
    chunk = outs // nlat
    width = cols + 2 * EDGE
    zero_border(xp, rows, nlat)
    own_g = pltpu.make_async_copy(g, gv, lsem.at[0])
    own_x = pltpu.make_async_copy(
        x, xp.at[pl.ds(RATE, rows), :, pl.ds(EDGE, cols)], lsem.at[1]
    )
    own_x.start()
    own_g.start()
    barrier = pltpu.get_barrier_semaphore()

    def hello(peer_lat, peer_lon):
        pl.semaphore_signal(barrier, inc=1, device_id=(peer_lat, peer_lon), device_id_type=MESH)

    def greet_lat(i, carry):
        hello(lax.rem(lat + i, nlat), lon)
        return carry

    def greet_lon(i, carry):
        hello(lat, lax.rem(lon + i, nlon))
        return carry

    lax.fori_loop(1, nlat, greet_lat, 0)
    lax.fori_loop(1, nlon, greet_lon, 0)
    for dr, dc in SIDES:
        if dr != 0 and dc != 0:
            ok = (lat + dr >= 0) & (lat + dr < nlat)
            pl.when(ok)(
                functools.partial(
                    hello, lax.rem(lat + dr + nlat, nlat), lax.rem(lon + dc + nlon, nlon)
                )
            )
    corners = 2 * (lat > 0).astype(jnp.int32) + 2 * (lat < nlat - 1).astype(jnp.int32)
    pl.semaphore_wait(barrier, nlat - 1 + nlon - 1 + corners)

    halo = halo_copies(x, xp, hsend, hrecv, nlat, nlon)
    halo_do(halo, "start")
    own_x.wait()
    own_g.wait()
    halo_do(halo, "wait_recv")

    def shift(r, carry):
        row = xp[r].astype(F32)
        xs[0, r] = pltpu.roll(row, RATE, 1)[:, EDGE : EDGE + cols].astype(BF16)
        xs[1, r] = row[:, EDGE : EDGE + cols].astype(BF16)
        xs[2, r] = pltpu.roll(row, width - RATE, 1)[:, EDGE : EDGE + cols].astype(BF16)
        return carry

    lax.fori_loop(0, rows + 2 * RATE, shift, 0)

    def taps(r):
        return jnp.concatenate(
            [xs[b, r + a * RATE] for a in range(3) for b in range(3)], axis=0
        )

    acc[...] = jnp.zeros_like(acc)

    def grad(r, carry):
        acc[...] += lax.dot_general(
            gv[r], taps(r), (((1,), (1,)), ((), ())), preferred_element_type=F32
        )
        return carry

    lax.fori_loop(0, rows, grad, 0)

    def forward(r, carry):
        feat[r] = jnp.dot(wf[...], taps(r), preferred_element_type=F32).astype(BF16)
        return carry

    def rows_of(which):
        return pl.ds(pl.multiple_of(which * chunk, chunk), chunk)

    def scatter(i, out):
        peer = lax.rem(lat + i, nlat) if out else lax.rem(lat + nlat - i, nlat)
        slot = lat if out else peer
        return pltpu.make_async_remote_copy(
            acc.at[rows_of(peer)], latbuf.at[slot], asend.at[i], arecv.at[slot],
            device_id=(peer, lon), device_id_type=MESH,
        )

    def swap(i, out):
        peer = lax.rem(lon + i, nlon) if out else lax.rem(lon + nlon - i, nlon)
        slot = lon if out else peer
        return pltpu.make_async_remote_copy(
            part, lonbuf.at[slot], bsend.at[i], brecv.at[slot],
            device_id=(lat, peer), device_id_type=MESH,
        )

    def collect(i, out):
        peer = lax.rem(lat + i, nlat) if out else lax.rem(lat + nlat - i, nlat)
        mine = lat if out else peer
        return pltpu.make_async_remote_copy(
            done.at[mine], done.at[mine], csend.at[i], crecv.at[mine],
            device_id=(peer, lon), device_id_type=MESH,
        )

    for i in range(1, nlat):
        scatter(i, True).start()
    latbuf[lat] = acc[rows_of(lat)]
    half = rows // 2
    lax.fori_loop(0, half, forward, 0)
    for i in range(1, nlat):
        scatter(i, False).wait_recv()
    part[...] = jnp.sum(latbuf[...], axis=0)
    for i in range(1, nlon):
        swap(i, True).start()
    lonbuf[lon] = part[...]
    lax.fori_loop(half, rows, forward, 0)
    for i in range(1, nlon):
        swap(i, False).wait_recv()
    done[lat] = jnp.sum(lonbuf[...], axis=0) * scale
    for i in range(1, nlat):
        collect(i, True).start()
    for i in range(1, nlat):
        scatter(i, True).wait_send()
    for i in range(1, nlon):
        swap(i, True).wait_send()
    halo_do(halo, "wait_send")
    for i in range(1, nlat):
        collect(i, False).wait_recv()
    dw[...] = done[...]
    for i in range(1, nlat):
        collect(i, True).wait_send()


VM = pl.BlockSpec(memory_space=pltpu.VMEM)
ANY = pl.BlockSpec(memory_space=pl.ANY)


def dmas(*counts):
    return [pltpu.SemaphoreType.DMA((count,)) for count in counts]


def local(
    source_elements, remap_weights, element_index, patch_index, block_counts, conv_weight, cotangent
):
    nlat, nlon = lax.axis_size("lat"), lax.axis_size("lon")
    local_weights = remap_weights[0]
    chosen = element_index[0]
    targets = patch_index[0]
    counts = block_counts[0]
    owners, cap, points, cells = local_weights.shape
    _, outs, nvars = conv_weight.shape
    rows, _, cols = cotangent.shape
    patches = rows * cols // cells
    element_rows = source_elements[chosen].reshape(owners, cap, points, nvars)
    blocks = jnp.einsum(
        "dkjc,dkjp->dkcp", element_rows, local_weights, preferred_element_type=F32
    ).astype(BF16)
    payload = blocks.reshape(owners, cap * nvars, cells)
    live = jnp.arange(cap, dtype=jnp.int32)[None, :] < counts[:, None]
    numbers = jnp.where(live, targets, patches)
    numbers = jnp.pad(numbers, ((0, 0), (0, 128 - cap)))[:, None, :]
    taps = conv_weight.reshape(3, 3, outs, nvars)
    wb = taps.transpose(1, 3, 0, 2).reshape(3 * nvars, 3 * outs)
    wf = taps.transpose(2, 0, 1, 3).reshape(outs, 9 * nvars)
    width = cols + 2 * EDGE
    arrived, arrived_numbers, input_grad = pl.pallas_call(
        functools.partial(exchange_kernel, nlat, nlon),
        out_shape=(
            jax.ShapeDtypeStruct(payload.shape, BF16),
            jax.ShapeDtypeStruct(numbers.shape, jnp.int32),
            jax.ShapeDtypeStruct((rows, nvars, cols), BF16),
        ),
        in_specs=[ANY, ANY, ANY, VM],
        out_specs=(ANY, ANY, VM),
        scratch_shapes=[pltpu.VMEM((rows + 2 * RATE, outs, width), BF16)]
        + dmas(owners, owners, owners, owners, 8, 8, 3),
        compiler_params=pltpu.CompilerParams(
            collective_id=0, has_side_effects=True, vmem_limit_bytes=32 << 20
        ),
    )(payload, numbers, cotangent, wb)
    remapped = pl.pallas_call(
        functools.partial(scatter_kernel, cap),
        out_shape=jax.ShapeDtypeStruct((rows, nvars, cols), BF16),
        in_specs=[pl.BlockSpec(memory_space=pltpu.SMEM), VM],
        out_specs=VM,
        scratch_shapes=[pltpu.VMEM((patches + 1, nvars, cells), F32)],
        compiler_params=pltpu.CompilerParams(vmem_limit_bytes=32 << 20),
    )(arrived_numbers, arrived)
    chunk = outs // nlat
    scale = 1.0 / math.sqrt(rows * cols * nlat * nlon)
    features, grads = pl.pallas_call(
        functools.partial(conv_kernel, nlat, nlon, scale),
        out_shape=(
            jax.ShapeDtypeStruct((rows, outs, cols), BF16),
            jax.ShapeDtypeStruct((nlat, chunk, 9 * nvars), F32),
        ),
        in_specs=[ANY, ANY, VM],
        out_specs=(VM, VM),
        scratch_shapes=[
            pltpu.VMEM((rows + 2 * RATE, nvars, width), BF16),
            pltpu.VMEM((3, rows + 2 * RATE, nvars, cols), BF16),
            pltpu.VMEM((rows, outs, cols), BF16),
            pltpu.VMEM((outs, 9 * nvars), F32),
            pltpu.VMEM((nlat, chunk, 9 * nvars), F32),
            pltpu.VMEM((chunk, 9 * nvars), F32),
            pltpu.VMEM((nlon, chunk, 9 * nvars), F32),
            pltpu.VMEM((nlat, chunk, 9 * nvars), F32),
        ]
        + dmas(8, 8, nlat, nlat, nlon, nlon, nlat, nlat, 2),
        compiler_params=pltpu.CompilerParams(
            collective_id=1, has_side_effects=True, vmem_limit_bytes=40 << 20
        ),
    )(remapped, cotangent, wf)
    weight_grad = grads.reshape(outs, 9, nvars).transpose(1, 0, 2)
    return features, input_grad, weight_grad


def solution(mesh):
    in_specs = (
        P(("lat", "lon"), None),
        P(("lat", "lon"), None, None, None, None),
        P(("lat", "lon"), None, None),
        P(("lat", "lon"), None, None),
        P(("lat", "lon"), None),
        P(),
        P("lat", None, "lon"),
    )
    out_specs = (P("lat", None, "lon"), P("lat", None, "lon"), P())
    return jax.shard_map(local, mesh=mesh, in_specs=in_specs, out_specs=out_specs, check_vma=False)
```

```python
import functools
import math

import jax
import jax.numpy as jnp
from jax import lax
from jax.experimental import pallas as pl
from jax.experimental.pallas import tpu as pltpu
from jax.sharding import PartitionSpec as P

RATE = 4
EDGE = 128
MESH = pl.DeviceIdType.MESH
F32 = jnp.float32
BF16 = jnp.bfloat16
SIDES = [(-1, -1), (-1, 0), (-1, 1), (0, -1), (0, 1), (1, -1), (1, 0), (1, 1)]


def span(step, total, width):
    before, size = width
    if step < 0:
        return (0, size), (before + total, size)
    if step > 0:
        return (total - size, size), (before - size, size)
    return (0, total), (before, total)


def halo_copies(field, padded, send, recv, nlat, nlon):
    lat, lon = lax.axis_index("lat"), lax.axis_index("lon")
    rows, _, cols = field.shape
    made = []
    for k, (dr, dc) in enumerate(SIDES):
        (r0, rn), (pr, _) = span(dr, rows, (RATE, RATE))
        (c0, cn), (pc, _) = span(dc, cols, (EDGE, EDGE))
        to_lat, from_lat = lat + dr, lat - dr
        copy = pltpu.make_async_remote_copy(
            src_ref=field.at[pl.ds(r0, rn), :, pl.ds(c0, cn)],
            dst_ref=padded.at[pl.ds(pr, rn), :, pl.ds(pc, cn)],
            send_sem=send.at[k],
            recv_sem=recv.at[k],
            device_id=(lax.rem(to_lat + nlat, nlat), lax.rem(lon + dc + nlon, nlon)),
            device_id_type=MESH,
        )
        sends = (to_lat >= 0) & (to_lat < nlat)
        gets = (from_lat >= 0) & (from_lat < nlat)
        made.append((dr, sends, gets, copy))
    return made


def halo_do(made, what):
    for dr, sends, gets, copy in made:
        cond = gets if what == "wait_recv" else sends
        act = getattr(copy, what)
        if dr == 0:
            act()
        else:
            pl.when(cond)(act)


def zero_border(padded, rows, nlat):
    lat = lax.axis_index("lat")

    @pl.when(lat == 0)
    def _():
        padded[0:RATE] = jnp.zeros((RATE,) + padded.shape[1:], padded.dtype)

    @pl.when(lat == nlat - 1)
    def _():
        padded[RATE + rows : 2 * RATE + rows] = jnp.zeros(
            (RATE,) + padded.shape[1:], padded.dtype
        )


def edge_copies(packed, landed, send, recv, nlat, nlon):
    lat, lon = lax.axis_index("lat"), lax.axis_index("lon")
    made = []
    for k, (dr, dc) in enumerate(SIDES):
        if dc == 0:
            continue
        to_lat, from_lat = lat + dr, lat - dr
        copy = pltpu.make_async_remote_copy(
            src_ref=packed.at[0 if dc < 0 else 1],
            dst_ref=landed.at[k],
            send_sem=send.at[k],
            recv_sem=recv.at[k],
            device_id=(lax.rem(to_lat + nlat, nlat), lax.rem(lon + dc + nlon, nlon)),
            device_id_type=MESH,
        )
        sends = (to_lat >= 0) & (to_lat < nlat)
        gets = (from_lat >= 0) & (from_lat < nlat)
        made.append((dr, sends, gets, copy))
    return made


def pack_edges(padded, packed, rows, cols):
    lane = lax.broadcasted_iota(jnp.int32, packed.shape[1:], 1)
    first = jnp.zeros(packed.shape[1:], F32)
    last = first
    for i in range(rows):
        here = (lane >= i * RATE) & (lane < (i + 1) * RATE)
        head = padded[RATE + i, :, EDGE : 2 * EDGE].astype(F32)
        tail = padded[RATE + i, :, cols : cols + EDGE].astype(F32)
        first = jnp.where(here, pltpu.roll(head, i * RATE, 1) if i else head, first)
        last = jnp.where(here, pltpu.roll(tail, (i + 1) * RATE, 1), last)
    packed[0] = first.astype(BF16)
    packed[1] = last.astype(BF16)


def unpack_edges(landed, padded, rows, cols, nlat):
    lat = lax.axis_index("lat")
    for k, (dr, dc) in enumerate(SIDES):
        if dc == 0:
            continue

        def place(k=k, dr=dr, dc=dc):
            block = landed[k].astype(F32)
            base = {-1: RATE + rows, 0: RATE, 1: RATE - rows}[dr]
            taken = {-1: range(RATE), 0: range(rows), 1: range(rows - RATE, rows)}[dr]
            for i in taken:
                move = (EDGE - i * RATE - (0 if dc < 0 else RATE)) % EDGE
                tile = (pltpu.roll(block, move, 1) if move else block).astype(BF16)
                if dc < 0:
                    padded[base + i, :, EDGE + cols : 2 * EDGE + cols] = tile
                else:
                    padded[base + i, :, 0:EDGE] = tile

        if dr == 0:
            place()
        else:
            pl.when((lat - dr >= 0) & (lat - dr < nlat))(place)


def exchange_kernel(
    nlat, nlon, pay, tgt, g, wb, arr, tarr, ig, gp, packed, landed, psend, precv, tsend, trecv, hsend, hrecv, lsem
):
    lat, lon = lax.axis_index("lat"), lax.axis_index("lon")
    n = nlat * nlon
    me = lat * nlon + lon
    rows, _, cols = g.shape
    nvars = ig.shape[1]
    zero_border(gp, rows, nlat)
    own_g = pltpu.make_async_copy(
        g, gp.at[pl.ds(RATE, rows), :, pl.ds(EDGE, cols)], lsem.at[0]
    )
    own_g.start()
    own_p = pltpu.make_async_copy(pay.at[me], arr.at[me], lsem.at[1])
    own_t = pltpu.make_async_copy(tgt.at[me], tarr.at[me], lsem.at[2])
    own_p.start()
    own_t.start()

    barrier = pltpu.get_barrier_semaphore()

    def greet(i, carry):
        peer = lax.rem(me + i, n)
        pl.semaphore_signal(
            barrier, inc=1, device_id=(peer // nlon, lax.rem(peer, nlon)), device_id_type=MESH
        )
        return carry

    lax.fori_loop(1, n, greet, 0)
    own_g.wait()
    pack_edges(gp, packed, rows, cols)
    pl.semaphore_wait(barrier, n - 1)

    def block(i, forward):
        peer = lax.rem(me + i, n) if forward else lax.rem(me + n - i, n)
        slot = me if forward else peer
        where = (peer // nlon, lax.rem(peer, nlon))
        return (
            pltpu.make_async_remote_copy(
                pay.at[peer], arr.at[slot], psend.at[i], precv.at[slot],
                device_id=where, device_id_type=MESH,
            ),
            pltpu.make_async_remote_copy(
                tgt.at[peer], tarr.at[slot], tsend.at[i], trecv.at[slot],
                device_id=where, device_id_type=MESH,
            ),
        )

    halo = [
        side
        for side, (_, dc) in zip(halo_copies(g, gp, hsend, hrecv, nlat, nlon), SIDES)
        if dc == 0
    ] + edge_copies(packed, landed, hsend, hrecv, nlat, nlon)

    def send(i, carry):
        data, number = block(i, True)
        number.start()
        data.start()
        return carry

    halo_do(halo, "start")
    lax.fori_loop(1, n, send, 0)
    halo_do(halo, "wait_recv")
    unpack_edges(landed, gp, rows, cols, nlat)

    def back(r, carry):
        stack = jnp.concatenate([gp[r + 2 * RATE], gp[r + RATE], gp[r]], axis=0)
        y = jnp.dot(wb[...], stack, preferred_element_type=F32)
        width = cols + 2 * EDGE
        low = pltpu.roll(y[0:nvars], width - RATE, 1)
        high = pltpu.roll(y[2 * nvars : 3 * nvars], RATE, 1)
        total = low + y[nvars : 2 * nvars] + high
        ig[r] = total[:, EDGE : EDGE + cols].astype(BF16)
        return carry

    lax.fori_loop(0, rows, back, 0)
    halo_do(halo, "wait_send")
    own_p.wait()
    own_t.wait()

    def finish(i, carry):
        data, number = block(i, False)
        number.wait_recv()
        data.wait_recv()
        number.wait_send()
        data.wait_send()
        return carry

    lax.fori_loop(1, n, finish, 0)


def scatter_kernel(cap, tgt, arr, x, acc):
    n = arr.shape[0]
    rows, nvars, cols = x.shape
    across = cols // EDGE
    acc[...] = jnp.zeros_like(acc)

    def add(s, carry):
        for j in range(cap):
            q = tgt[s, 0, j]
            acc[q] = acc[q] + arr[s, j * nvars : (j + 1) * nvars, :].astype(F32)
        return carry

    lax.fori_loop(0, n, add, 0)

    def store(r, carry):
        for c in range(across):
            x[r, :, c * EDGE : (c + 1) * EDGE] = acc[r * across + c].astype(BF16)
        return carry

    lax.fori_loop(0, rows, store, 0)


def conv_kernel(
    nlat, nlon, scale, x, g, wf, feat, dw,
    xp, xs, gv, acc, latbuf, part, lonbuf, done,
    hsend, hrecv, asend, arecv, bsend, brecv, csend, crecv, lsem,
):
    lat, lon = lax.axis_index("lat"), lax.axis_index("lon")
    rows, nvars, cols = x.shape
    outs = g.shape[1]
    chunk = outs // nlat
    width = cols + 2 * EDGE
    zero_border(xp, rows, nlat)
    own_g = pltpu.make_async_copy(g, gv, lsem.at[0])
    own_x = pltpu.make_async_copy(
        x, xp.at[pl.ds(RATE, rows), :, pl.ds(EDGE, cols)], lsem.at[1]
    )
    own_x.start()
    own_g.start()
    barrier = pltpu.get_barrier_semaphore()

    def hello(peer_lat, peer_lon):
        pl.semaphore_signal(barrier, inc=1, device_id=(peer_lat, peer_lon), device_id_type=MESH)

    def greet_lat(i, carry):
        hello(lax.rem(lat + i, nlat), lon)
        return carry

    def greet_lon(i, carry):
        hello(lat, lax.rem(lon + i, nlon))
        return carry

    lax.fori_loop(1, nlat, greet_lat, 0)
    lax.fori_loop(1, nlon, greet_lon, 0)
    for dr, dc in SIDES:
        if dr != 0 and dc != 0:
            ok = (lat + dr >= 0) & (lat + dr < nlat)
            pl.when(ok)(
                functools.partial(
                    hello, lax.rem(lat + dr + nlat, nlat), lax.rem(lon + dc + nlon, nlon)
                )
            )
    corners = 2 * (lat > 0).astype(jnp.int32) + 2 * (lat < nlat - 1).astype(jnp.int32)
    pl.semaphore_wait(barrier, nlat - 1 + nlon - 1 + corners)

    halo = halo_copies(x, xp, hsend, hrecv, nlat, nlon)
    halo_do(halo, "start")
    own_x.wait()
    own_g.wait()
    halo_do(halo, "wait_recv")

    def shift(r, carry):
        row = xp[r].astype(F32)
        xs[0, r] = pltpu.roll(row, RATE, 1)[:, EDGE : EDGE + cols].astype(BF16)
        xs[1, r] = row[:, EDGE : EDGE + cols].astype(BF16)
        xs[2, r] = pltpu.roll(row, width - RATE, 1)[:, EDGE : EDGE + cols].astype(BF16)
        return carry

    lax.fori_loop(0, rows + 2 * RATE, shift, 0)

    def taps(r):
        return jnp.concatenate(
            [xs[b, r + a * RATE] for a in range(3) for b in range(3)], axis=0
        )

    acc[...] = jnp.zeros_like(acc)

    def grad(r, carry):
        acc[...] += lax.dot_general(
            gv[r], taps(r), (((1,), (1,)), ((), ())), preferred_element_type=F32
        )
        return carry

    lax.fori_loop(0, rows, grad, 0)

    def forward(r, carry):
        feat[r] = jnp.dot(wf[...], taps(r), preferred_element_type=F32).astype(BF16)
        return carry

    def rows_of(which):
        return pl.ds(pl.multiple_of(which * chunk, chunk), chunk)

    def scatter(i, out):
        peer = lax.rem(lat + i, nlat) if out else lax.rem(lat + nlat - i, nlat)
        slot = lat if out else peer
        return pltpu.make_async_remote_copy(
            acc.at[rows_of(peer)], latbuf.at[slot], asend.at[i], arecv.at[slot],
            device_id=(peer, lon), device_id_type=MESH,
        )

    def swap(i, out):
        peer = lax.rem(lon + i, nlon) if out else lax.rem(lon + nlon - i, nlon)
        slot = lon if out else peer
        return pltpu.make_async_remote_copy(
            part, lonbuf.at[slot], bsend.at[i], brecv.at[slot],
            device_id=(lat, peer), device_id_type=MESH,
        )

    def collect(i, out):
        peer = lax.rem(lat + i, nlat) if out else lax.rem(lat + nlat - i, nlat)
        mine = lat if out else peer
        return pltpu.make_async_remote_copy(
            done.at[mine], done.at[mine], csend.at[i], crecv.at[mine],
            device_id=(peer, lon), device_id_type=MESH,
        )

    for i in range(1, nlat):
        scatter(i, True).start()
    latbuf[lat] = acc[rows_of(lat)]
    half = rows // 2
    lax.fori_loop(0, half, forward, 0)
    for i in range(1, nlat):
        scatter(i, False).wait_recv()
    part[...] = jnp.sum(latbuf[...], axis=0)
    for i in range(1, nlon):
        swap(i, True).start()
    lonbuf[lon] = part[...]
    lax.fori_loop(half, rows, forward, 0)
    for i in range(1, nlon):
        swap(i, False).wait_recv()
    done[lat] = jnp.sum(lonbuf[...], axis=0) * scale
    for i in range(1, nlat):
        collect(i, True).start()
    for i in range(1, nlat):
        scatter(i, True).wait_send()
    for i in range(1, nlon):
        swap(i, True).wait_send()
    halo_do(halo, "wait_send")
    for i in range(1, nlat):
        collect(i, False).wait_recv()
    dw[...] = done[...]
    for i in range(1, nlat):
        collect(i, True).wait_send()


VM = pl.BlockSpec(memory_space=pltpu.VMEM)
ANY = pl.BlockSpec(memory_space=pl.ANY)


def dmas(*counts):
    return [pltpu.SemaphoreType.DMA((count,)) for count in counts]


def local(
    source_elements, remap_weights, element_index, patch_index, block_counts, conv_weight, cotangent
):
    nlat, nlon = lax.axis_size("lat"), lax.axis_size("lon")
    local_weights = remap_weights[0]
    chosen = element_index[0]
    targets = patch_index[0]
    counts = block_counts[0]
    owners, cap, points, cells = local_weights.shape
    _, outs, nvars = conv_weight.shape
    rows, _, cols = cotangent.shape
    patches = rows * cols // cells
    element_rows = source_elements[chosen].reshape(owners, cap, points, nvars)
    blocks = jnp.einsum(
        "dkjc,dkjp->dkcp", element_rows, local_weights, preferred_element_type=F32
    ).astype(BF16)
    payload = blocks.reshape(owners, cap * nvars, cells)
    live = jnp.arange(cap, dtype=jnp.int32)[None, :] < counts[:, None]
    numbers = jnp.where(live, targets, patches)
    numbers = jnp.pad(numbers, ((0, 0), (0, 128 - cap)))[:, None, :]
    taps = conv_weight.reshape(3, 3, outs, nvars)
    wb = taps.transpose(1, 3, 0, 2).reshape(3 * nvars, 3 * outs)
    wf = taps.transpose(2, 0, 1, 3).reshape(outs, 9 * nvars)
    width = cols + 2 * EDGE
    arrived, arrived_numbers, input_grad = pl.pallas_call(
        functools.partial(exchange_kernel, nlat, nlon),
        out_shape=(
            jax.ShapeDtypeStruct(payload.shape, BF16),
            jax.ShapeDtypeStruct(numbers.shape, jnp.int32),
            jax.ShapeDtypeStruct((rows, nvars, cols), BF16),
        ),
        in_specs=[ANY, ANY, ANY, VM],
        out_specs=(ANY, ANY, VM),
        scratch_shapes=[
            pltpu.VMEM((rows + 2 * RATE, outs, width), BF16),
            pltpu.VMEM((2, outs, EDGE), BF16),
            pltpu.VMEM((8, outs, EDGE), BF16),
        ]
        + dmas(owners, owners, owners, owners, 8, 8, 3),
        compiler_params=pltpu.CompilerParams(
            collective_id=0, has_side_effects=True, vmem_limit_bytes=32 << 20
        ),
    )(payload, numbers, cotangent, wb)
    remapped = pl.pallas_call(
        functools.partial(scatter_kernel, cap),
        out_shape=jax.ShapeDtypeStruct((rows, nvars, cols), BF16),
        in_specs=[pl.BlockSpec(memory_space=pltpu.SMEM), VM],
        out_specs=VM,
        scratch_shapes=[pltpu.VMEM((patches + 1, nvars, cells), F32)],
        compiler_params=pltpu.CompilerParams(vmem_limit_bytes=32 << 20),
    )(arrived_numbers, arrived)
    chunk = outs // nlat
    scale = 1.0 / math.sqrt(rows * cols * nlat * nlon)
    features, grads = pl.pallas_call(
        functools.partial(conv_kernel, nlat, nlon, scale),
        out_shape=(
            jax.ShapeDtypeStruct((rows, outs, cols), BF16),
            jax.ShapeDtypeStruct((nlat, chunk, 9 * nvars), F32),
        ),
        in_specs=[ANY, ANY, VM],
        out_specs=(VM, VM),
        scratch_shapes=[
            pltpu.VMEM((rows + 2 * RATE, nvars, width), BF16),
            pltpu.VMEM((3, rows + 2 * RATE, nvars, cols), BF16),
            pltpu.VMEM((rows, outs, cols), BF16),
            pltpu.VMEM((outs, 9 * nvars), F32),
            pltpu.VMEM((nlat, chunk, 9 * nvars), F32),
            pltpu.VMEM((chunk, 9 * nvars), F32),
            pltpu.VMEM((nlon, chunk, 9 * nvars), F32),
            pltpu.VMEM((nlat, chunk, 9 * nvars), F32),
        ]
        + dmas(8, 8, nlat, nlat, nlon, nlon, nlat, nlat, 2),
        compiler_params=pltpu.CompilerParams(
            collective_id=1, has_side_effects=True, vmem_limit_bytes=40 << 20
        ),
    )(remapped, cotangent, wf)
    weight_grad = grads.reshape(outs, 9, nvars).transpose(1, 0, 2)
    return features, input_grad, weight_grad


def solution(mesh):
    in_specs = (
        P(("lat", "lon"), None),
        P(("lat", "lon"), None, None, None, None),
        P(("lat", "lon"), None, None),
        P(("lat", "lon"), None, None),
        P(("lat", "lon"), None),
        P(),
        P("lat", None, "lon"),
    )
    out_specs = (P("lat", None, "lon"), P("lat", None, "lon"), P())
    return jax.shard_map(local, mesh=mesh, in_specs=in_specs, out_specs=out_specs, check_vma=False)
```

```python
import functools
import math

import jax
import jax.numpy as jnp
from jax import lax
from jax.experimental import pallas as pl
from jax.experimental.pallas import tpu as pltpu
from jax.sharding import PartitionSpec as P

RATE = 4
EDGE = 128
MESH = pl.DeviceIdType.MESH
F32 = jnp.float32
BF16 = jnp.bfloat16
SIDES = [(-1, -1), (-1, 0), (-1, 1), (0, -1), (0, 1), (1, -1), (1, 0), (1, 1)]


def span(step, total, width):
    before, size = width
    if step < 0:
        return (0, size), (before + total, size)
    if step > 0:
        return (total - size, size), (before - size, size)
    return (0, total), (before, total)


def halo_copies(field, padded, send, recv, nlat, nlon):
    lat, lon = lax.axis_index("lat"), lax.axis_index("lon")
    rows, _, cols = field.shape
    made = []
    for k, (dr, dc) in enumerate(SIDES):
        (r0, rn), (pr, _) = span(dr, rows, (RATE, RATE))
        (c0, cn), (pc, _) = span(dc, cols, (EDGE, EDGE))
        to_lat, from_lat = lat + dr, lat - dr
        copy = pltpu.make_async_remote_copy(
            src_ref=field.at[pl.ds(r0, rn), :, pl.ds(c0, cn)],
            dst_ref=padded.at[pl.ds(pr, rn), :, pl.ds(pc, cn)],
            send_sem=send.at[k],
            recv_sem=recv.at[k],
            device_id=(lax.rem(to_lat + nlat, nlat), lax.rem(lon + dc + nlon, nlon)),
            device_id_type=MESH,
        )
        sends = (to_lat >= 0) & (to_lat < nlat)
        gets = (from_lat >= 0) & (from_lat < nlat)
        made.append((dr, sends, gets, copy))
    return made


def halo_do(made, what):
    for dr, sends, gets, copy in made:
        cond = gets if what == "wait_recv" else sends
        act = getattr(copy, what)
        if dr == 0:
            act()
        else:
            pl.when(cond)(act)


def zero_border(padded, rows, nlat):
    lat = lax.axis_index("lat")

    @pl.when(lat == 0)
    def _():
        padded[0:RATE] = jnp.zeros((RATE,) + padded.shape[1:], padded.dtype)

    @pl.when(lat == nlat - 1)
    def _():
        padded[RATE + rows : 2 * RATE + rows] = jnp.zeros(
            (RATE,) + padded.shape[1:], padded.dtype
        )


def edge_copies(packed, landed, send, recv, nlat, nlon):
    lat, lon = lax.axis_index("lat"), lax.axis_index("lon")
    made = []
    for k, (dr, dc) in enumerate(SIDES):
        if dc == 0:
            continue
        to_lat, from_lat = lat + dr, lat - dr
        copy = pltpu.make_async_remote_copy(
            src_ref=packed.at[0 if dc < 0 else 1],
            dst_ref=landed.at[k],
            send_sem=send.at[k],
            recv_sem=recv.at[k],
            device_id=(lax.rem(to_lat + nlat, nlat), lax.rem(lon + dc + nlon, nlon)),
            device_id_type=MESH,
        )
        sends = (to_lat >= 0) & (to_lat < nlat)
        gets = (from_lat >= 0) & (from_lat < nlat)
        made.append((dr, sends, gets, copy))
    return made


def pack_edges(padded, packed, rows, cols):
    lane = lax.broadcasted_iota(jnp.int32, packed.shape[1:], 1)
    first = jnp.zeros(packed.shape[1:], F32)
    last = first
    for i in range(rows):
        here = (lane >= i * RATE) & (lane < (i + 1) * RATE)
        head = padded[RATE + i, :, EDGE : 2 * EDGE].astype(F32)
        tail = padded[RATE + i, :, cols : cols + EDGE].astype(F32)
        first = jnp.where(here, pltpu.roll(head, i * RATE, 1) if i else head, first)
        last = jnp.where(here, pltpu.roll(tail, (i + 1) * RATE, 1), last)
    packed[0] = first.astype(BF16)
    packed[1] = last.astype(BF16)


def unpack_edges(landed, padded, rows, cols, nlat):
    lat = lax.axis_index("lat")
    for k, (dr, dc) in enumerate(SIDES):
        if dc == 0:
            continue

        def place(k=k, dr=dr, dc=dc):
            block = landed[k].astype(F32)
            base = {-1: RATE + rows, 0: RATE, 1: RATE - rows}[dr]
            taken = {-1: range(RATE), 0: range(rows), 1: range(rows - RATE, rows)}[dr]
            for i in taken:
                move = (EDGE - i * RATE - (0 if dc < 0 else RATE)) % EDGE
                tile = (pltpu.roll(block, move, 1) if move else block).astype(BF16)
                if dc < 0:
                    padded[base + i, :, EDGE + cols : 2 * EDGE + cols] = tile
                else:
                    padded[base + i, :, 0:EDGE] = tile

        if dr == 0:
            place()
        else:
            pl.when((lat - dr >= 0) & (lat - dr < nlat))(place)


def exchange_kernel(
    nlat, nlon, pay, tgt, g, wb, arr, tarr, ig, gp, packed, landed, psend, precv, tsend, trecv, hsend, hrecv, lsem
):
    lat, lon = lax.axis_index("lat"), lax.axis_index("lon")
    n = nlat * nlon
    me = lat * nlon + lon
    rows, _, cols = g.shape
    nvars = ig.shape[1]
    zero_border(gp, rows, nlat)
    own_g = pltpu.make_async_copy(
        g, gp.at[pl.ds(RATE, rows), :, pl.ds(EDGE, cols)], lsem.at[0]
    )
    own_g.start()
    own_p = pltpu.make_async_copy(pay.at[me], arr.at[me], lsem.at[1])
    own_t = pltpu.make_async_copy(tgt.at[me], tarr.at[me], lsem.at[2])
    own_p.start()
    own_t.start()

    barrier = pltpu.get_barrier_semaphore()

    def greet(i, carry):
        peer = lax.rem(me + i, n)
        pl.semaphore_signal(
            barrier, inc=1, device_id=(peer // nlon, lax.rem(peer, nlon)), device_id_type=MESH
        )
        return carry

    lax.fori_loop(1, n, greet, 0)
    own_g.wait()
    pack_edges(gp, packed, rows, cols)
    pl.semaphore_wait(barrier, n - 1)

    def block(i, forward):
        peer = lax.rem(me + i, n) if forward else lax.rem(me + n - i, n)
        slot = me if forward else peer
        where = (peer // nlon, lax.rem(peer, nlon))
        return (
            pltpu.make_async_remote_copy(
                pay.at[peer], arr.at[slot], psend.at[i], precv.at[slot],
                device_id=where, device_id_type=MESH,
            ),
            pltpu.make_async_remote_copy(
                tgt.at[peer], tarr.at[slot], tsend.at[i], trecv.at[slot],
                device_id=where, device_id_type=MESH,
            ),
        )

    halo = [
        side
        for side, (_, dc) in zip(halo_copies(g, gp, hsend, hrecv, nlat, nlon), SIDES)
        if dc == 0
    ] + edge_copies(packed, landed, hsend, hrecv, nlat, nlon)

    def send(i, carry):
        data, number = block(i, True)
        number.start()
        data.start()
        return carry

    halo_do(halo, "start")
    lax.fori_loop(1, n, send, 0)
    halo_do(halo, "wait_recv")
    unpack_edges(landed, gp, rows, cols, nlat)

    def back(r, carry):
        stack = jnp.concatenate([gp[r + 2 * RATE], gp[r + RATE], gp[r]], axis=0)
        y = jnp.dot(wb[...], stack, preferred_element_type=F32)
        width = cols + 2 * EDGE
        low = pltpu.roll(y[0:nvars], width - RATE, 1)
        high = pltpu.roll(y[2 * nvars : 3 * nvars], RATE, 1)
        total = low + y[nvars : 2 * nvars] + high
        ig[r] = total[:, EDGE : EDGE + cols].astype(BF16)
        return carry

    lax.fori_loop(0, rows, back, 0)
    halo_do(halo, "wait_send")
    own_p.wait()
    own_t.wait()

    def finish(i, carry):
        data, number = block(i, False)
        number.wait_recv()
        data.wait_recv()
        number.wait_send()
        data.wait_send()
        return carry

    lax.fori_loop(1, n, finish, 0)


def scatter_kernel(cap, tgt, arr, x, acc):
    n = arr.shape[0]
    rows, nvars, cols = x.shape
    across = cols // EDGE
    acc[...] = jnp.zeros_like(acc)

    def add(s, carry):
        for j in range(cap):
            q = tgt[s, 0, j]
            acc[q] = acc[q] + arr[s, j * nvars : (j + 1) * nvars, :].astype(F32)
        return carry

    lax.fori_loop(0, n, add, 0)

    def store(r, carry):
        for c in range(across):
            x[r, :, c * EDGE : (c + 1) * EDGE] = acc[r * across + c].astype(BF16)
        return carry

    lax.fori_loop(0, rows, store, 0)


def conv_kernel(
    nlat, nlon, scale, x, g, wf, feat, dw,
    xp, packed, landed, xs, gv, acc, latbuf, part, lonbuf, done,
    hsend, hrecv, asend, arecv, bsend, brecv, csend, crecv, lsem,
):
    lat, lon = lax.axis_index("lat"), lax.axis_index("lon")
    rows, nvars, cols = x.shape
    outs = g.shape[1]
    chunk = outs // nlat
    width = cols + 2 * EDGE
    zero_border(xp, rows, nlat)
    own_g = pltpu.make_async_copy(g, gv, lsem.at[0])
    own_x = pltpu.make_async_copy(
        x, xp.at[pl.ds(RATE, rows), :, pl.ds(EDGE, cols)], lsem.at[1]
    )
    own_x.start()
    own_g.start()
    barrier = pltpu.get_barrier_semaphore()

    def hello(peer_lat, peer_lon):
        pl.semaphore_signal(barrier, inc=1, device_id=(peer_lat, peer_lon), device_id_type=MESH)

    def greet_lat(i, carry):
        hello(lax.rem(lat + i, nlat), lon)
        return carry

    def greet_lon(i, carry):
        hello(lat, lax.rem(lon + i, nlon))
        return carry

    lax.fori_loop(1, nlat, greet_lat, 0)
    lax.fori_loop(1, nlon, greet_lon, 0)
    for dr, dc in SIDES:
        if dr != 0 and dc != 0:
            ok = (lat + dr >= 0) & (lat + dr < nlat)
            pl.when(ok)(
                functools.partial(
                    hello, lax.rem(lat + dr + nlat, nlat), lax.rem(lon + dc + nlon, nlon)
                )
            )
    own_x.wait()
    pack_edges(xp, packed, rows, cols)
    corners = 2 * (lat > 0).astype(jnp.int32) + 2 * (lat < nlat - 1).astype(jnp.int32)
    pl.semaphore_wait(barrier, nlat - 1 + nlon - 1 + corners)

    halo = [
        side
        for side, (_, dc) in zip(halo_copies(x, xp, hsend, hrecv, nlat, nlon), SIDES)
        if dc == 0
    ] + edge_copies(packed, landed, hsend, hrecv, nlat, nlon)
    halo_do(halo, "start")
    own_g.wait()
    halo_do(halo, "wait_recv")
    unpack_edges(landed, xp, rows, cols, nlat)

    def shift(r, carry):
        row = xp[r].astype(F32)
        xs[0, r] = pltpu.roll(row, RATE, 1)[:, EDGE : EDGE + cols].astype(BF16)
        xs[1, r] = row[:, EDGE : EDGE + cols].astype(BF16)
        xs[2, r] = pltpu.roll(row, width - RATE, 1)[:, EDGE : EDGE + cols].astype(BF16)
        return carry

    lax.fori_loop(0, rows + 2 * RATE, shift, 0)

    def taps(r):
        return jnp.concatenate(
            [xs[b, r + a * RATE] for a in range(3) for b in range(3)], axis=0
        )

    acc[...] = jnp.zeros_like(acc)

    def grad(r, carry):
        acc[...] += lax.dot_general(
            gv[r], taps(r), (((1,), (1,)), ((), ())), preferred_element_type=F32
        )
        return carry

    lax.fori_loop(0, rows, grad, 0)

    def forward(r, carry):
        feat[r] = jnp.dot(wf[...], taps(r), preferred_element_type=F32).astype(BF16)
        return carry

    def rows_of(which):
        return pl.ds(pl.multiple_of(which * chunk, chunk), chunk)

    def scatter(i, out):
        peer = lax.rem(lat + i, nlat) if out else lax.rem(lat + nlat - i, nlat)
        slot = lat if out else peer
        return pltpu.make_async_remote_copy(
            acc.at[rows_of(peer)], latbuf.at[slot], asend.at[i], arecv.at[slot],
            device_id=(peer, lon), device_id_type=MESH,
        )

    def swap(i, out):
        peer = lax.rem(lon + i, nlon) if out else lax.rem(lon + nlon - i, nlon)
        slot = lon if out else peer
        return pltpu.make_async_remote_copy(
            part, lonbuf.at[slot], bsend.at[i], brecv.at[slot],
            device_id=(lat, peer), device_id_type=MESH,
        )

    def collect(i, out):
        peer = lax.rem(lat + i, nlat) if out else lax.rem(lat + nlat - i, nlat)
        mine = lat if out else peer
        return pltpu.make_async_remote_copy(
            done.at[mine], done.at[mine], csend.at[i], crecv.at[mine],
            device_id=(peer, lon), device_id_type=MESH,
        )

    for i in range(1, nlat):
        scatter(i, True).start()
    latbuf[lat] = acc[rows_of(lat)]
    half = rows // 2
    lax.fori_loop(0, half, forward, 0)
    for i in range(1, nlat):
        scatter(i, False).wait_recv()
    part[...] = jnp.sum(latbuf[...], axis=0)
    for i in range(1, nlon):
        swap(i, True).start()
    lonbuf[lon] = part[...]
    lax.fori_loop(half, rows, forward, 0)
    for i in range(1, nlon):
        swap(i, False).wait_recv()
    done[lat] = jnp.sum(lonbuf[...], axis=0) * scale
    for i in range(1, nlat):
        collect(i, True).start()
    for i in range(1, nlat):
        scatter(i, True).wait_send()
    for i in range(1, nlon):
        swap(i, True).wait_send()
    halo_do(halo, "wait_send")
    for i in range(1, nlat):
        collect(i, False).wait_recv()
    dw[...] = done[...]
    for i in range(1, nlat):
        collect(i, True).wait_send()


VM = pl.BlockSpec(memory_space=pltpu.VMEM)
ANY = pl.BlockSpec(memory_space=pl.ANY)


def dmas(*counts):
    return [pltpu.SemaphoreType.DMA((count,)) for count in counts]


def local(
    source_elements, remap_weights, element_index, patch_index, block_counts, conv_weight, cotangent
):
    nlat, nlon = lax.axis_size("lat"), lax.axis_size("lon")
    local_weights = remap_weights[0]
    chosen = element_index[0]
    targets = patch_index[0]
    counts = block_counts[0]
    owners, cap, points, cells = local_weights.shape
    _, outs, nvars = conv_weight.shape
    rows, _, cols = cotangent.shape
    patches = rows * cols // cells
    element_rows = source_elements[chosen].reshape(owners, cap, points, nvars)
    blocks = jnp.einsum(
        "dkjc,dkjp->dkcp", element_rows, local_weights, preferred_element_type=F32
    ).astype(BF16)
    payload = blocks.reshape(owners, cap * nvars, cells)
    live = jnp.arange(cap, dtype=jnp.int32)[None, :] < counts[:, None]
    numbers = jnp.where(live, targets, patches)
    numbers = jnp.pad(numbers, ((0, 0), (0, 128 - cap)))[:, None, :]
    taps = conv_weight.reshape(3, 3, outs, nvars)
    wb = taps.transpose(1, 3, 0, 2).reshape(3 * nvars, 3 * outs)
    wf = taps.transpose(2, 0, 1, 3).reshape(outs, 9 * nvars)
    width = cols + 2 * EDGE
    arrived, arrived_numbers, input_grad = pl.pallas_call(
        functools.partial(exchange_kernel, nlat, nlon),
        out_shape=(
            jax.ShapeDtypeStruct(payload.shape, BF16),
            jax.ShapeDtypeStruct(numbers.shape, jnp.int32),
            jax.ShapeDtypeStruct((rows, nvars, cols), BF16),
        ),
        in_specs=[ANY, ANY, ANY, VM],
        out_specs=(ANY, ANY, VM),
        scratch_shapes=[
            pltpu.VMEM((rows + 2 * RATE, outs, width), BF16),
            pltpu.VMEM((2, outs, EDGE), BF16),
            pltpu.VMEM((8, outs, EDGE), BF16),
        ]
        + dmas(owners, owners, owners, owners, 8, 8, 3),
        compiler_params=pltpu.CompilerParams(
            collective_id=0, has_side_effects=True, vmem_limit_bytes=32 << 20
        ),
    )(payload, numbers, cotangent, wb)
    remapped = pl.pallas_call(
        functools.partial(scatter_kernel, cap),
        out_shape=jax.ShapeDtypeStruct((rows, nvars, cols), BF16),
        in_specs=[pl.BlockSpec(memory_space=pltpu.SMEM), VM],
        out_specs=VM,
        scratch_shapes=[pltpu.VMEM((patches + 1, nvars, cells), F32)],
        compiler_params=pltpu.CompilerParams(vmem_limit_bytes=32 << 20),
    )(arrived_numbers, arrived)
    chunk = outs // nlat
    scale = 1.0 / math.sqrt(rows * cols * nlat * nlon)
    features, grads = pl.pallas_call(
        functools.partial(conv_kernel, nlat, nlon, scale),
        out_shape=(
            jax.ShapeDtypeStruct((rows, outs, cols), BF16),
            jax.ShapeDtypeStruct((nlat, chunk, 9 * nvars), F32),
        ),
        in_specs=[ANY, ANY, VM],
        out_specs=(VM, VM),
        scratch_shapes=[
            pltpu.VMEM((rows + 2 * RATE, nvars, width), BF16),
            pltpu.VMEM((2, nvars, EDGE), BF16),
            pltpu.VMEM((8, nvars, EDGE), BF16),
            pltpu.VMEM((3, rows + 2 * RATE, nvars, cols), BF16),
            pltpu.VMEM((rows, outs, cols), BF16),
            pltpu.VMEM((outs, 9 * nvars), F32),
            pltpu.VMEM((nlat, chunk, 9 * nvars), F32),
            pltpu.VMEM((chunk, 9 * nvars), F32),
            pltpu.VMEM((nlon, chunk, 9 * nvars), F32),
            pltpu.VMEM((nlat, chunk, 9 * nvars), F32),
        ]
        + dmas(8, 8, nlat, nlat, nlon, nlon, nlat, nlat, 2),
        compiler_params=pltpu.CompilerParams(
            collective_id=1, has_side_effects=True, vmem_limit_bytes=40 << 20
        ),
    )(remapped, cotangent, wf)
    weight_grad = grads.reshape(outs, 9, nvars).transpose(1, 0, 2)
    return features, input_grad, weight_grad


def solution(mesh):
    in_specs = (
        P(("lat", "lon"), None),
        P(("lat", "lon"), None, None, None, None),
        P(("lat", "lon"), None, None),
        P(("lat", "lon"), None, None),
        P(("lat", "lon"), None),
        P(),
        P("lat", None, "lon"),
    )
    out_specs = (P("lat", None, "lon"), P("lat", None, "lon"), P())
    return jax.shard_map(local, mesh=mesh, in_specs=in_specs, out_specs=out_specs, check_vma=False)
```

```python
import functools
import math

import jax
import jax.numpy as jnp
from jax import lax
from jax.experimental import pallas as pl
from jax.experimental.pallas import tpu as pltpu
from jax.sharding import PartitionSpec as P

RATE = 4
EDGE = 128
MESH = pl.DeviceIdType.MESH
F32 = jnp.float32
BF16 = jnp.bfloat16
SIDES = [(-1, -1), (-1, 0), (-1, 1), (0, -1), (0, 1), (1, -1), (1, 0), (1, 1)]


def span(step, total, width):
    before, size = width
    if step < 0:
        return (0, size), (before + total, size)
    if step > 0:
        return (total - size, size), (before - size, size)
    return (0, total), (before, total)


def halo_copies(field, padded, send, recv, nlat, nlon):
    lat, lon = lax.axis_index("lat"), lax.axis_index("lon")
    rows, _, cols = field.shape
    made = []
    for k, (dr, dc) in enumerate(SIDES):
        (r0, rn), (pr, _) = span(dr, rows, (RATE, RATE))
        (c0, cn), (pc, _) = span(dc, cols, (EDGE, EDGE))
        to_lat, from_lat = lat + dr, lat - dr
        copy = pltpu.make_async_remote_copy(
            src_ref=field.at[pl.ds(r0, rn), :, pl.ds(c0, cn)],
            dst_ref=padded.at[pl.ds(pr, rn), :, pl.ds(pc, cn)],
            send_sem=send.at[k],
            recv_sem=recv.at[k],
            device_id=(lax.rem(to_lat + nlat, nlat), lax.rem(lon + dc + nlon, nlon)),
            device_id_type=MESH,
        )
        sends = (to_lat >= 0) & (to_lat < nlat)
        gets = (from_lat >= 0) & (from_lat < nlat)
        made.append((dr, sends, gets, copy))
    return made


def halo_do(made, what):
    for dr, sends, gets, copy in made:
        cond = gets if what == "wait_recv" else sends
        act = getattr(copy, what)
        if dr == 0:
            act()
        else:
            pl.when(cond)(act)


def zero_border(padded, rows, nlat):
    lat = lax.axis_index("lat")

    @pl.when(lat == 0)
    def _():
        padded[0:RATE] = jnp.zeros((RATE,) + padded.shape[1:], padded.dtype)

    @pl.when(lat == nlat - 1)
    def _():
        padded[RATE + rows : 2 * RATE + rows] = jnp.zeros(
            (RATE,) + padded.shape[1:], padded.dtype
        )


def edge_copies(packed, landed, send, recv, nlat, nlon):
    lat, lon = lax.axis_index("lat"), lax.axis_index("lon")
    made = []
    for k, (dr, dc) in enumerate(SIDES):
        if dc == 0:
            continue
        to_lat, from_lat = lat + dr, lat - dr
        copy = pltpu.make_async_remote_copy(
            src_ref=packed.at[0 if dc < 0 else 1],
            dst_ref=landed.at[k],
            send_sem=send.at[k],
            recv_sem=recv.at[k],
            device_id=(lax.rem(to_lat + nlat, nlat), lax.rem(lon + dc + nlon, nlon)),
            device_id_type=MESH,
        )
        sends = (to_lat >= 0) & (to_lat < nlat)
        gets = (from_lat >= 0) & (from_lat < nlat)
        made.append((dr, sends, gets, copy))
    return made


def pack_edges(padded, packed, rows, cols):
    lane = lax.broadcasted_iota(jnp.int32, packed.shape[1:], 1)
    first = jnp.zeros(packed.shape[1:], F32)
    last = first
    for i in range(rows):
        here = (lane >= i * RATE) & (lane < (i + 1) * RATE)
        head = padded[RATE + i, :, EDGE : 2 * EDGE].astype(F32)
        tail = padded[RATE + i, :, cols : cols + EDGE].astype(F32)
        first = jnp.where(here, pltpu.roll(head, i * RATE, 1) if i else head, first)
        last = jnp.where(here, pltpu.roll(tail, (i + 1) * RATE, 1), last)
    packed[0] = first.astype(BF16)
    packed[1] = last.astype(BF16)


def unpack_edges(landed, padded, rows, cols, nlat):
    lat = lax.axis_index("lat")
    for k, (dr, dc) in enumerate(SIDES):
        if dc == 0:
            continue

        def place(k=k, dr=dr, dc=dc):
            block = landed[k].astype(F32)
            base = {-1: RATE + rows, 0: RATE, 1: RATE - rows}[dr]
            taken = {-1: range(RATE), 0: range(rows), 1: range(rows - RATE, rows)}[dr]
            for i in taken:
                move = (EDGE - i * RATE - (0 if dc < 0 else RATE)) % EDGE
                tile = (pltpu.roll(block, move, 1) if move else block).astype(BF16)
                if dc < 0:
                    padded[base + i, :, EDGE + cols : 2 * EDGE + cols] = tile
                else:
                    padded[base + i, :, 0:EDGE] = tile

        if dr == 0:
            place()
        else:
            pl.when((lat - dr >= 0) & (lat - dr < nlat))(place)


def exchange_kernel(
    nlat, nlon, pay, tgt, g, wb, arr, tarr, ig, gp, packed, landed, psend, precv, tsend, trecv, hsend, hrecv, lsem
):
    lat, lon = lax.axis_index("lat"), lax.axis_index("lon")
    n = nlat * nlon
    me = lat * nlon + lon
    rows, _, cols = g.shape
    nvars = ig.shape[1]
    zero_border(gp, rows, nlat)
    own_g = pltpu.make_async_copy(
        g, gp.at[pl.ds(RATE, rows), :, pl.ds(EDGE, cols)], lsem.at[0]
    )
    own_g.start()
    own_p = pltpu.make_async_copy(pay.at[me], arr.at[me], lsem.at[1])
    own_t = pltpu.make_async_copy(tgt.at[me], tarr.at[me], lsem.at[2])
    own_p.start()
    own_t.start()

    barrier = pltpu.get_barrier_semaphore()

    def greet(i, carry):
        peer = lax.rem(me + i, n)
        pl.semaphore_signal(
            barrier, inc=1, device_id=(peer // nlon, lax.rem(peer, nlon)), device_id_type=MESH
        )
        return carry

    lax.fori_loop(1, n, greet, 0)
    own_g.wait()
    pack_edges(gp, packed, rows, cols)
    pl.semaphore_wait(barrier, n - 1)

    def block(i, forward):
        peer = lax.rem(me + i, n) if forward else lax.rem(me + n - i, n)
        slot = me if forward else peer
        where = (peer // nlon, lax.rem(peer, nlon))
        return (
            pltpu.make_async_remote_copy(
                pay.at[peer], arr.at[slot], psend.at[i], precv.at[slot],
                device_id=where, device_id_type=MESH,
            ),
            pltpu.make_async_remote_copy(
                tgt.at[peer], tarr.at[slot], tsend.at[i], trecv.at[slot],
                device_id=where, device_id_type=MESH,
            ),
        )

    halo = [
        side
        for side, (_, dc) in zip(halo_copies(g, gp, hsend, hrecv, nlat, nlon), SIDES)
        if dc == 0
    ] + edge_copies(packed, landed, hsend, hrecv, nlat, nlon)

    def send(i, carry):
        data, number = block(i, True)
        number.start()
        data.start()
        return carry

    halo_do(halo, "start")
    lax.fori_loop(1, n, send, 0)
    halo_do(halo, "wait_recv")
    unpack_edges(landed, gp, rows, cols, nlat)

    def back(r, carry):
        stack = jnp.concatenate([gp[r + 2 * RATE], gp[r + RATE], gp[r]], axis=0)
        y = jnp.dot(wb[...], stack, preferred_element_type=F32)
        width = cols + 2 * EDGE
        low = pltpu.roll(y[0:nvars], width - RATE, 1)
        high = pltpu.roll(y[2 * nvars : 3 * nvars], RATE, 1)
        total = low + y[nvars : 2 * nvars] + high
        ig[r] = total[:, EDGE : EDGE + cols].astype(BF16)
        return carry

    lax.fori_loop(0, rows, back, 0)
    halo_do(halo, "wait_send")
    own_p.wait()
    own_t.wait()

    def finish(i, carry):
        data, number = block(i, False)
        number.wait_recv()
        data.wait_recv()
        number.wait_send()
        data.wait_send()
        return carry

    lax.fori_loop(1, n, finish, 0)


def scatter_kernel(cap, tgt, arr, x, acc):
    n = arr.shape[0]
    rows, nvars, cols = x.shape
    across = cols // EDGE
    acc[...] = jnp.zeros_like(acc)

    def add(s, carry):
        for j in range(cap):
            q = tgt[s, 0, j]
            acc[q] = acc[q] + arr[s, j * nvars : (j + 1) * nvars, :].astype(F32)
        return carry

    lax.fori_loop(0, n, add, 0)

    def store(r, carry):
        for c in range(across):
            x[r, :, c * EDGE : (c + 1) * EDGE] = acc[r * across + c].astype(BF16)
        return carry

    lax.fori_loop(0, rows, store, 0)


def conv_kernel(
    nlat, nlon, scale, x, g, wf, feat, dw,
    xp, packed, landed, xs, gv, acc, latbuf, part, lonbuf, done,
    hsend, hrecv, asend, arecv, bsend, brecv, csend, crecv, lsem,
):
    lat, lon = lax.axis_index("lat"), lax.axis_index("lon")
    rows, nvars, cols = x.shape
    outs = g.shape[1]
    chunk = outs // nlat
    width = cols + 2 * EDGE
    zero_border(xp, rows, nlat)
    own_g = pltpu.make_async_copy(g, gv, lsem.at[0])
    own_x = pltpu.make_async_copy(
        x, xp.at[pl.ds(RATE, rows), :, pl.ds(EDGE, cols)], lsem.at[1]
    )
    own_x.start()
    own_g.start()
    barrier = pltpu.get_barrier_semaphore()

    def hello(peer_lat, peer_lon):
        pl.semaphore_signal(barrier, inc=1, device_id=(peer_lat, peer_lon), device_id_type=MESH)

    def greet_lat(i, carry):
        hello(lax.rem(lat + i, nlat), lon)
        return carry

    def greet_lon(i, carry):
        hello(lat, lax.rem(lon + i, nlon))
        return carry

    lax.fori_loop(1, nlat, greet_lat, 0)
    lax.fori_loop(1, nlon, greet_lon, 0)
    for dr, dc in SIDES:
        if dr != 0 and dc != 0:
            ok = (lat + dr >= 0) & (lat + dr < nlat)
            pl.when(ok)(
                functools.partial(
                    hello, lax.rem(lat + dr + nlat, nlat), lax.rem(lon + dc + nlon, nlon)
                )
            )
    own_x.wait()
    pack_edges(xp, packed, rows, cols)
    corners = 2 * (lat > 0).astype(jnp.int32) + 2 * (lat < nlat - 1).astype(jnp.int32)
    pl.semaphore_wait(barrier, nlat - 1 + nlon - 1 + corners)

    halo = [
        side
        for side, (_, dc) in zip(halo_copies(x, xp, hsend, hrecv, nlat, nlon), SIDES)
        if dc == 0
    ] + edge_copies(packed, landed, hsend, hrecv, nlat, nlon)
    halo_do(halo, "start")
    own_g.wait()
    halo_do(halo, "wait_recv")
    unpack_edges(landed, xp, rows, cols, nlat)

    def shift(r, carry):
        row = xp[r].astype(F32)
        xs[0, r] = pltpu.roll(row, RATE, 1)[:, EDGE : EDGE + cols].astype(BF16)
        xs[1, r] = row[:, EDGE : EDGE + cols].astype(BF16)
        xs[2, r] = pltpu.roll(row, width - RATE, 1)[:, EDGE : EDGE + cols].astype(BF16)
        return carry

    lax.fori_loop(0, rows + 2 * RATE, shift, 0, unroll=4)

    def taps(r):
        return jnp.concatenate(
            [xs[b, r + a * RATE] for a in range(3) for b in range(3)], axis=0
        )

    acc[...] = jnp.zeros_like(acc)

    def grad(r, carry):
        acc[...] += lax.dot_general(
            gv[r], taps(r), (((1,), (1,)), ((), ())), preferred_element_type=F32
        )
        return carry

    lax.fori_loop(0, rows, grad, 0, unroll=4)

    def forward(r, carry):
        feat[r] = jnp.dot(wf[...], taps(r), preferred_element_type=F32).astype(BF16)
        return carry

    def rows_of(which):
        return pl.ds(pl.multiple_of(which * chunk, chunk), chunk)

    def scatter(i, out):
        peer = lax.rem(lat + i, nlat) if out else lax.rem(lat + nlat - i, nlat)
        slot = lat if out else peer
        return pltpu.make_async_remote_copy(
            acc.at[rows_of(peer)], latbuf.at[slot], asend.at[i], arecv.at[slot],
            device_id=(peer, lon), device_id_type=MESH,
        )

    def swap(i, out):
        peer = lax.rem(lon + i, nlon) if out else lax.rem(lon + nlon - i, nlon)
        slot = lon if out else peer
        return pltpu.make_async_remote_copy(
            part, lonbuf.at[slot], bsend.at[i], brecv.at[slot],
            device_id=(lat, peer), device_id_type=MESH,
        )

    def collect(i, out):
        peer = lax.rem(lat + i, nlat) if out else lax.rem(lat + nlat - i, nlat)
        mine = lat if out else peer
        return pltpu.make_async_remote_copy(
            done.at[mine], done.at[mine], csend.at[i], crecv.at[mine],
            device_id=(peer, lon), device_id_type=MESH,
        )

    for i in range(1, nlat):
        scatter(i, True).start()
    latbuf[lat] = acc[rows_of(lat)]
    half = rows // 2
    lax.fori_loop(0, half, forward, 0)
    for i in range(1, nlat):
        scatter(i, False).wait_recv()
    part[...] = jnp.sum(latbuf[...], axis=0)
    for i in range(1, nlon):
        swap(i, True).start()
    lonbuf[lon] = part[...]
    lax.fori_loop(half, rows, forward, 0)
    for i in range(1, nlon):
        swap(i, False).wait_recv()
    done[lat] = jnp.sum(lonbuf[...], axis=0) * scale
    for i in range(1, nlat):
        collect(i, True).start()
    for i in range(1, nlat):
        scatter(i, True).wait_send()
    for i in range(1, nlon):
        swap(i, True).wait_send()
    halo_do(halo, "wait_send")
    for i in range(1, nlat):
        collect(i, False).wait_recv()
    dw[...] = done[...]
    for i in range(1, nlat):
        collect(i, True).wait_send()


VM = pl.BlockSpec(memory_space=pltpu.VMEM)
ANY = pl.BlockSpec(memory_space=pl.ANY)


def dmas(*counts):
    return [pltpu.SemaphoreType.DMA((count,)) for count in counts]


def local(
    source_elements, remap_weights, element_index, patch_index, block_counts, conv_weight, cotangent
):
    nlat, nlon = lax.axis_size("lat"), lax.axis_size("lon")
    local_weights = remap_weights[0]
    chosen = element_index[0]
    targets = patch_index[0]
    counts = block_counts[0]
    owners, cap, points, cells = local_weights.shape
    _, outs, nvars = conv_weight.shape
    rows, _, cols = cotangent.shape
    patches = rows * cols // cells
    element_rows = source_elements[chosen].reshape(owners, cap, points, nvars)
    blocks = jnp.einsum(
        "dkjc,dkjp->dkcp", element_rows, local_weights, preferred_element_type=F32
    ).astype(BF16)
    payload = blocks.reshape(owners, cap * nvars, cells)
    live = jnp.arange(cap, dtype=jnp.int32)[None, :] < counts[:, None]
    numbers = jnp.where(live, targets, patches)
    numbers = jnp.pad(numbers, ((0, 0), (0, 128 - cap)))[:, None, :]
    taps = conv_weight.reshape(3, 3, outs, nvars)
    wb = taps.transpose(1, 3, 0, 2).reshape(3 * nvars, 3 * outs)
    wf = taps.transpose(2, 0, 1, 3).reshape(outs, 9 * nvars)
    width = cols + 2 * EDGE
    arrived, arrived_numbers, input_grad = pl.pallas_call(
        functools.partial(exchange_kernel, nlat, nlon),
        out_shape=(
            jax.ShapeDtypeStruct(payload.shape, BF16),
            jax.ShapeDtypeStruct(numbers.shape, jnp.int32),
            jax.ShapeDtypeStruct((rows, nvars, cols), BF16),
        ),
        in_specs=[ANY, ANY, ANY, VM],
        out_specs=(ANY, ANY, VM),
        scratch_shapes=[
            pltpu.VMEM((rows + 2 * RATE, outs, width), BF16),
            pltpu.VMEM((2, outs, EDGE), BF16),
            pltpu.VMEM((8, outs, EDGE), BF16),
        ]
        + dmas(owners, owners, owners, owners, 8, 8, 3),
        compiler_params=pltpu.CompilerParams(
            collective_id=0, has_side_effects=True, vmem_limit_bytes=32 << 20
        ),
    )(payload, numbers, cotangent, wb)
    remapped = pl.pallas_call(
        functools.partial(scatter_kernel, cap),
        out_shape=jax.ShapeDtypeStruct((rows, nvars, cols), BF16),
        in_specs=[pl.BlockSpec(memory_space=pltpu.SMEM), VM],
        out_specs=VM,
        scratch_shapes=[pltpu.VMEM((patches + 1, nvars, cells), F32)],
        compiler_params=pltpu.CompilerParams(vmem_limit_bytes=32 << 20),
    )(arrived_numbers, arrived)
    chunk = outs // nlat
    scale = 1.0 / math.sqrt(rows * cols * nlat * nlon)
    features, grads = pl.pallas_call(
        functools.partial(conv_kernel, nlat, nlon, scale),
        out_shape=(
            jax.ShapeDtypeStruct((rows, outs, cols), BF16),
            jax.ShapeDtypeStruct((nlat, chunk, 9 * nvars), F32),
        ),
        in_specs=[ANY, ANY, VM],
        out_specs=(VM, VM),
        scratch_shapes=[
            pltpu.VMEM((rows + 2 * RATE, nvars, width), BF16),
            pltpu.VMEM((2, nvars, EDGE), BF16),
            pltpu.VMEM((8, nvars, EDGE), BF16),
            pltpu.VMEM((3, rows + 2 * RATE, nvars, cols), BF16),
            pltpu.VMEM((rows, outs, cols), BF16),
            pltpu.VMEM((outs, 9 * nvars), F32),
            pltpu.VMEM((nlat, chunk, 9 * nvars), F32),
            pltpu.VMEM((chunk, 9 * nvars), F32),
            pltpu.VMEM((nlon, chunk, 9 * nvars), F32),
            pltpu.VMEM((nlat, chunk, 9 * nvars), F32),
        ]
        + dmas(8, 8, nlat, nlat, nlon, nlon, nlat, nlat, 2),
        compiler_params=pltpu.CompilerParams(
            collective_id=1, has_side_effects=True, vmem_limit_bytes=40 << 20
        ),
    )(remapped, cotangent, wf)
    weight_grad = grads.reshape(outs, 9, nvars).transpose(1, 0, 2)
    return features, input_grad, weight_grad


def solution(mesh):
    in_specs = (
        P(("lat", "lon"), None),
        P(("lat", "lon"), None, None, None, None),
        P(("lat", "lon"), None, None),
        P(("lat", "lon"), None, None),
        P(("lat", "lon"), None),
        P(),
        P("lat", None, "lon"),
    )
    out_specs = (P("lat", None, "lon"), P("lat", None, "lon"), P())
    return jax.shard_map(local, mesh=mesh, in_specs=in_specs, out_specs=out_specs, check_vma=False)
```

```python
import functools
import math

import jax
import jax.numpy as jnp
from jax import lax
from jax.experimental import pallas as pl
from jax.experimental.pallas import tpu as pltpu
from jax.sharding import PartitionSpec as P

RATE = 4
EDGE = 128
MESH = pl.DeviceIdType.MESH
F32 = jnp.float32
BF16 = jnp.bfloat16
SIDES = [(-1, -1), (-1, 0), (-1, 1), (0, -1), (0, 1), (1, -1), (1, 0), (1, 1)]


def span(step, total, width):
    before, size = width
    if step < 0:
        return (0, size), (before + total, size)
    if step > 0:
        return (total - size, size), (before - size, size)
    return (0, total), (before, total)


def halo_copies(field, padded, send, recv, nlat, nlon):
    lat, lon = lax.axis_index("lat"), lax.axis_index("lon")
    rows, _, cols = field.shape
    made = []
    for k, (dr, dc) in enumerate(SIDES):
        (r0, rn), (pr, _) = span(dr, rows, (RATE, RATE))
        (c0, cn), (pc, _) = span(dc, cols, (EDGE, EDGE))
        to_lat, from_lat = lat + dr, lat - dr
        copy = pltpu.make_async_remote_copy(
            src_ref=field.at[pl.ds(r0, rn), :, pl.ds(c0, cn)],
            dst_ref=padded.at[pl.ds(pr, rn), :, pl.ds(pc, cn)],
            send_sem=send.at[k],
            recv_sem=recv.at[k],
            device_id=(lax.rem(to_lat + nlat, nlat), lax.rem(lon + dc + nlon, nlon)),
            device_id_type=MESH,
        )
        sends = (to_lat >= 0) & (to_lat < nlat)
        gets = (from_lat >= 0) & (from_lat < nlat)
        made.append((dr, sends, gets, copy))
    return made


def halo_do(made, what):
    for dr, sends, gets, copy in made:
        cond = gets if what == "wait_recv" else sends
        act = getattr(copy, what)
        if dr == 0:
            act()
        else:
            pl.when(cond)(act)


def zero_border(padded, rows, nlat):
    lat = lax.axis_index("lat")

    @pl.when(lat == 0)
    def _():
        padded[0:RATE] = jnp.zeros((RATE,) + padded.shape[1:], padded.dtype)

    @pl.when(lat == nlat - 1)
    def _():
        padded[RATE + rows : 2 * RATE + rows] = jnp.zeros(
            (RATE,) + padded.shape[1:], padded.dtype
        )


def edge_copies(packed, landed, send, recv, nlat, nlon):
    lat, lon = lax.axis_index("lat"), lax.axis_index("lon")
    made = []
    for k, (dr, dc) in enumerate(SIDES):
        if dc == 0:
            continue
        to_lat, from_lat = lat + dr, lat - dr
        copy = pltpu.make_async_remote_copy(
            src_ref=packed.at[0 if dc < 0 else 1],
            dst_ref=landed.at[k],
            send_sem=send.at[k],
            recv_sem=recv.at[k],
            device_id=(lax.rem(to_lat + nlat, nlat), lax.rem(lon + dc + nlon, nlon)),
            device_id_type=MESH,
        )
        sends = (to_lat >= 0) & (to_lat < nlat)
        gets = (from_lat >= 0) & (from_lat < nlat)
        made.append((dr, sends, gets, copy))
    return made


def pack_edges(padded, packed, rows, cols):
    lane = lax.broadcasted_iota(jnp.int32, packed.shape[1:], 1)
    first = jnp.zeros(packed.shape[1:], F32)
    last = first
    for i in range(rows):
        here = (lane >= i * RATE) & (lane < (i + 1) * RATE)
        head = padded[RATE + i, :, EDGE : 2 * EDGE].astype(F32)
        tail = padded[RATE + i, :, cols : cols + EDGE].astype(F32)
        first = jnp.where(here, pltpu.roll(head, i * RATE, 1) if i else head, first)
        last = jnp.where(here, pltpu.roll(tail, (i + 1) * RATE, 1), last)
    packed[0] = first.astype(BF16)
    packed[1] = last.astype(BF16)


def unpack_edges(landed, padded, rows, cols, nlat, steps=(-1, 0, 1)):
    lat = lax.axis_index("lat")
    for k, (dr, dc) in enumerate(SIDES):
        if dc == 0 or dr not in steps:
            continue

        def place(k=k, dr=dr, dc=dc):
            block = landed[k].astype(F32)
            base = {-1: RATE + rows, 0: RATE, 1: RATE - rows}[dr]
            taken = {-1: range(RATE), 0: range(rows), 1: range(rows - RATE, rows)}[dr]
            for i in taken:
                move = (EDGE - i * RATE - (0 if dc < 0 else RATE)) % EDGE
                tile = (pltpu.roll(block, move, 1) if move else block).astype(BF16)
                if dc < 0:
                    padded[base + i, :, EDGE + cols : 2 * EDGE + cols] = tile
                else:
                    padded[base + i, :, 0:EDGE] = tile

        if dr == 0:
            place()
        else:
            pl.when((lat - dr >= 0) & (lat - dr < nlat))(place)


def exchange_kernel(
    nlat, nlon, pay, tgt, g, wb, arr, tarr, ig, gp, packed, landed, psend, precv, tsend, trecv, hsend, hrecv, lsem
):
    lat, lon = lax.axis_index("lat"), lax.axis_index("lon")
    n = nlat * nlon
    me = lat * nlon + lon
    rows, _, cols = g.shape
    nvars = ig.shape[1]
    zero_border(gp, rows, nlat)
    own_g = pltpu.make_async_copy(
        g, gp.at[pl.ds(RATE, rows), :, pl.ds(EDGE, cols)], lsem.at[0]
    )
    own_g.start()
    own_p = pltpu.make_async_copy(pay.at[me], arr.at[me], lsem.at[1])
    own_t = pltpu.make_async_copy(tgt.at[me], tarr.at[me], lsem.at[2])
    own_p.start()
    own_t.start()

    barrier = pltpu.get_barrier_semaphore()

    def greet(i, carry):
        peer = lax.rem(me + i, n)
        pl.semaphore_signal(
            barrier, inc=1, device_id=(peer // nlon, lax.rem(peer, nlon)), device_id_type=MESH
        )
        return carry

    lax.fori_loop(1, n, greet, 0)
    own_g.wait()
    pack_edges(gp, packed, rows, cols)
    pl.semaphore_wait(barrier, n - 1)

    def block(i, forward):
        peer = lax.rem(me + i, n) if forward else lax.rem(me + n - i, n)
        slot = me if forward else peer
        where = (peer // nlon, lax.rem(peer, nlon))
        return (
            pltpu.make_async_remote_copy(
                pay.at[peer], arr.at[slot], psend.at[i], precv.at[slot],
                device_id=where, device_id_type=MESH,
            ),
            pltpu.make_async_remote_copy(
                tgt.at[peer], tarr.at[slot], tsend.at[i], trecv.at[slot],
                device_id=where, device_id_type=MESH,
            ),
        )

    halo = [
        side
        for side, (_, dc) in zip(halo_copies(g, gp, hsend, hrecv, nlat, nlon), SIDES)
        if dc == 0
    ] + edge_copies(packed, landed, hsend, hrecv, nlat, nlon)

    def send(i, carry):
        data, number = block(i, True)
        number.start()
        data.start()
        return carry

    halo_do(halo, "start")
    lax.fori_loop(1, n, send, 0)
    halo_do(halo, "wait_recv")
    unpack_edges(landed, gp, rows, cols, nlat)

    def back(r, carry):
        stack = jnp.concatenate([gp[r + 2 * RATE], gp[r + RATE], gp[r]], axis=0)
        y = jnp.dot(wb[...], stack, preferred_element_type=F32)
        width = cols + 2 * EDGE
        low = pltpu.roll(y[0:nvars], width - RATE, 1)
        high = pltpu.roll(y[2 * nvars : 3 * nvars], RATE, 1)
        total = low + y[nvars : 2 * nvars] + high
        ig[r] = total[:, EDGE : EDGE + cols].astype(BF16)
        return carry

    lax.fori_loop(0, rows, back, 0)
    halo_do(halo, "wait_send")
    own_p.wait()
    own_t.wait()

    def finish(i, carry):
        data, number = block(i, False)
        number.wait_recv()
        data.wait_recv()
        number.wait_send()
        data.wait_send()
        return carry

    lax.fori_loop(1, n, finish, 0)


def scatter_kernel(cap, tgt, arr, x, acc):
    n = arr.shape[0]
    rows, nvars, cols = x.shape
    across = cols // EDGE
    acc[...] = jnp.zeros_like(acc)

    def add(s, carry):
        for j in range(cap):
            q = tgt[s, 0, j]
            acc[q] = acc[q] + arr[s, j * nvars : (j + 1) * nvars, :].astype(F32)
        return carry

    lax.fori_loop(0, n, add, 0)

    def store(r, carry):
        for c in range(across):
            x[r, :, c * EDGE : (c + 1) * EDGE] = acc[r * across + c].astype(BF16)
        return carry

    lax.fori_loop(0, rows, store, 0)


def conv_kernel(
    nlat, nlon, scale, x, g, wf, feat, dw,
    xp, packed, landed, xs, gv, acc, latbuf, part, lonbuf, done,
    hsend, hrecv, asend, arecv, bsend, brecv, csend, crecv, lsem,
):
    lat, lon = lax.axis_index("lat"), lax.axis_index("lon")
    rows, nvars, cols = x.shape
    outs = g.shape[1]
    chunk = outs // nlat
    width = cols + 2 * EDGE
    zero_border(xp, rows, nlat)
    own_g = pltpu.make_async_copy(g, gv, lsem.at[0])
    own_x = pltpu.make_async_copy(
        x, xp.at[pl.ds(RATE, rows), :, pl.ds(EDGE, cols)], lsem.at[1]
    )
    own_x.start()
    own_g.start()
    barrier = pltpu.get_barrier_semaphore()

    def hello(peer_lat, peer_lon):
        pl.semaphore_signal(barrier, inc=1, device_id=(peer_lat, peer_lon), device_id_type=MESH)

    def greet_lat(i, carry):
        hello(lax.rem(lat + i, nlat), lon)
        return carry

    def greet_lon(i, carry):
        hello(lat, lax.rem(lon + i, nlon))
        return carry

    lax.fori_loop(1, nlat, greet_lat, 0)
    lax.fori_loop(1, nlon, greet_lon, 0)
    for dr, dc in SIDES:
        if dr != 0 and dc != 0:
            ok = (lat + dr >= 0) & (lat + dr < nlat)
            pl.when(ok)(
                functools.partial(
                    hello, lax.rem(lat + dr + nlat, nlat), lax.rem(lon + dc + nlon, nlon)
                )
            )
    own_x.wait()
    pack_edges(xp, packed, rows, cols)
    corners = 2 * (lat > 0).astype(jnp.int32) + 2 * (lat < nlat - 1).astype(jnp.int32)
    pl.semaphore_wait(barrier, nlat - 1 + nlon - 1 + corners)

    halo = [
        side
        for side, (_, dc) in zip(halo_copies(x, xp, hsend, hrecv, nlat, nlon), SIDES)
        if dc == 0
    ] + edge_copies(packed, landed, hsend, hrecv, nlat, nlon)
    halo_do(halo, "start")
    own_g.wait()
    near = [side for side in halo if side[0] == 0]
    far = [side for side in halo if side[0] != 0]
    halo_do(near, "wait_recv")
    unpack_edges(landed, xp, rows, cols, nlat, (0,))

    def shift(r, carry):
        row = xp[r].astype(F32)
        xs[0, r] = pltpu.roll(row, RATE, 1)[:, EDGE : EDGE + cols].astype(BF16)
        xs[1, r] = row[:, EDGE : EDGE + cols].astype(BF16)
        xs[2, r] = pltpu.roll(row, width - RATE, 1)[:, EDGE : EDGE + cols].astype(BF16)
        return carry

    lax.fori_loop(RATE, rows + RATE, shift, 0, unroll=4)

    def taps(r):
        return jnp.concatenate(
            [xs[b, r + a * RATE] for a in range(3) for b in range(3)], axis=0
        )

    acc[...] = jnp.zeros_like(acc)

    def grad(r, carry):
        acc[...] += lax.dot_general(
            gv[r], taps(r), (((1,), (1,)), ((), ())), preferred_element_type=F32
        )
        return carry

    lax.fori_loop(RATE, rows - RATE, grad, 0, unroll=4)
    halo_do(far, "wait_recv")
    unpack_edges(landed, xp, rows, cols, nlat, (-1, 1))
    lax.fori_loop(0, RATE, shift, 0, unroll=4)
    lax.fori_loop(rows + RATE, rows + 2 * RATE, shift, 0, unroll=4)
    lax.fori_loop(0, RATE, grad, 0, unroll=4)
    lax.fori_loop(rows - RATE, rows, grad, 0, unroll=4)

    def forward(r, carry):
        feat[r] = jnp.dot(wf[...], taps(r), preferred_element_type=F32).astype(BF16)
        return carry

    def rows_of(which):
        return pl.ds(pl.multiple_of(which * chunk, chunk), chunk)

    def scatter(i, out):
        peer = lax.rem(lat + i, nlat) if out else lax.rem(lat + nlat - i, nlat)
        slot = lat if out else peer
        return pltpu.make_async_remote_copy(
            acc.at[rows_of(peer)], latbuf.at[slot], asend.at[i], arecv.at[slot],
            device_id=(peer, lon), device_id_type=MESH,
        )

    def swap(i, out):
        peer = lax.rem(lon + i, nlon) if out else lax.rem(lon + nlon - i, nlon)
        slot = lon if out else peer
        return pltpu.make_async_remote_copy(
            part, lonbuf.at[slot], bsend.at[i], brecv.at[slot],
            device_id=(lat, peer), device_id_type=MESH,
        )

    def collect(i, out):
        peer = lax.rem(lat + i, nlat) if out else lax.rem(lat + nlat - i, nlat)
        mine = lat if out else peer
        return pltpu.make_async_remote_copy(
            done.at[mine], done.at[mine], csend.at[i], crecv.at[mine],
            device_id=(peer, lon), device_id_type=MESH,
        )

    for i in range(1, nlat):
        scatter(i, True).start()
    latbuf[lat] = acc[rows_of(lat)]
    half = rows // 2
    lax.fori_loop(0, half, forward, 0)
    for i in range(1, nlat):
        scatter(i, False).wait_recv()
    part[...] = jnp.sum(latbuf[...], axis=0)
    for i in range(1, nlon):
        swap(i, True).start()
    lonbuf[lon] = part[...]
    lax.fori_loop(half, rows, forward, 0)
    for i in range(1, nlon):
        swap(i, False).wait_recv()
    done[lat] = jnp.sum(lonbuf[...], axis=0) * scale
    for i in range(1, nlat):
        collect(i, True).start()
    for i in range(1, nlat):
        scatter(i, True).wait_send()
    for i in range(1, nlon):
        swap(i, True).wait_send()
    halo_do(halo, "wait_send")
    for i in range(1, nlat):
        collect(i, False).wait_recv()
    dw[...] = done[...]
    for i in range(1, nlat):
        collect(i, True).wait_send()


VM = pl.BlockSpec(memory_space=pltpu.VMEM)
ANY = pl.BlockSpec(memory_space=pl.ANY)


def dmas(*counts):
    return [pltpu.SemaphoreType.DMA((count,)) for count in counts]


def local(
    source_elements, remap_weights, element_index, patch_index, block_counts, conv_weight, cotangent
):
    nlat, nlon = lax.axis_size("lat"), lax.axis_size("lon")
    local_weights = remap_weights[0]
    chosen = element_index[0]
    targets = patch_index[0]
    counts = block_counts[0]
    owners, cap, points, cells = local_weights.shape
    _, outs, nvars = conv_weight.shape
    rows, _, cols = cotangent.shape
    patches = rows * cols // cells
    element_rows = source_elements[chosen].reshape(owners, cap, points, nvars)
    blocks = jnp.einsum(
        "dkjc,dkjp->dkcp", element_rows, local_weights, preferred_element_type=F32
    ).astype(BF16)
    payload = blocks.reshape(owners, cap * nvars, cells)
    live = jnp.arange(cap, dtype=jnp.int32)[None, :] < counts[:, None]
    numbers = jnp.where(live, targets, patches)
    numbers = jnp.pad(numbers, ((0, 0), (0, 128 - cap)))[:, None, :]
    taps = conv_weight.reshape(3, 3, outs, nvars)
    wb = taps.transpose(1, 3, 0, 2).reshape(3 * nvars, 3 * outs)
    wf = taps.transpose(2, 0, 1, 3).reshape(outs, 9 * nvars)
    width = cols + 2 * EDGE
    arrived, arrived_numbers, input_grad = pl.pallas_call(
        functools.partial(exchange_kernel, nlat, nlon),
        out_shape=(
            jax.ShapeDtypeStruct(payload.shape, BF16),
            jax.ShapeDtypeStruct(numbers.shape, jnp.int32),
            jax.ShapeDtypeStruct((rows, nvars, cols), BF16),
        ),
        in_specs=[ANY, ANY, ANY, VM],
        out_specs=(ANY, ANY, VM),
        scratch_shapes=[
            pltpu.VMEM((rows + 2 * RATE, outs, width), BF16),
            pltpu.VMEM((2, outs, EDGE), BF16),
            pltpu.VMEM((8, outs, EDGE), BF16),
        ]
        + dmas(owners, owners, owners, owners, 8, 8, 3),
        compiler_params=pltpu.CompilerParams(
            collective_id=0, has_side_effects=True, vmem_limit_bytes=32 << 20
        ),
    )(payload, numbers, cotangent, wb)
    remapped = pl.pallas_call(
        functools.partial(scatter_kernel, cap),
        out_shape=jax.ShapeDtypeStruct((rows, nvars, cols), BF16),
        in_specs=[pl.BlockSpec(memory_space=pltpu.SMEM), VM],
        out_specs=VM,
        scratch_shapes=[pltpu.VMEM((patches + 1, nvars, cells), F32)],
        compiler_params=pltpu.CompilerParams(vmem_limit_bytes=32 << 20),
    )(arrived_numbers, arrived)
    chunk = outs // nlat
    scale = 1.0 / math.sqrt(rows * cols * nlat * nlon)
    features, grads = pl.pallas_call(
        functools.partial(conv_kernel, nlat, nlon, scale),
        out_shape=(
            jax.ShapeDtypeStruct((rows, outs, cols), BF16),
            jax.ShapeDtypeStruct((nlat, chunk, 9 * nvars), F32),
        ),
        in_specs=[ANY, ANY, VM],
        out_specs=(VM, VM),
        scratch_shapes=[
            pltpu.VMEM((rows + 2 * RATE, nvars, width), BF16),
            pltpu.VMEM((2, nvars, EDGE), BF16),
            pltpu.VMEM((8, nvars, EDGE), BF16),
            pltpu.VMEM((3, rows + 2 * RATE, nvars, cols), BF16),
            pltpu.VMEM((rows, outs, cols), BF16),
            pltpu.VMEM((outs, 9 * nvars), F32),
            pltpu.VMEM((nlat, chunk, 9 * nvars), F32),
            pltpu.VMEM((chunk, 9 * nvars), F32),
            pltpu.VMEM((nlon, chunk, 9 * nvars), F32),
            pltpu.VMEM((nlat, chunk, 9 * nvars), F32),
        ]
        + dmas(8, 8, nlat, nlat, nlon, nlon, nlat, nlat, 2),
        compiler_params=pltpu.CompilerParams(
            collective_id=1, has_side_effects=True, vmem_limit_bytes=40 << 20
        ),
    )(remapped, cotangent, wf)
    weight_grad = grads.reshape(outs, 9, nvars).transpose(1, 0, 2)
    return features, input_grad, weight_grad


def solution(mesh):
    in_specs = (
        P(("lat", "lon"), None),
        P(("lat", "lon"), None, None, None, None),
        P(("lat", "lon"), None, None),
        P(("lat", "lon"), None, None),
        P(("lat", "lon"), None),
        P(),
        P("lat", None, "lon"),
    )
    out_specs = (P("lat", None, "lon"), P("lat", None, "lon"), P())
    return jax.shard_map(local, mesh=mesh, in_specs=in_specs, out_specs=out_specs, check_vma=False)
```
